32 devices in a mesh: gx: 4 (over x, core), gy: 2 (over y), gz: 4 (over z).
Axes of the slice: x: 2, y: 2, z: 4, core: 2. Of those that a mesh axis runs over, the one named last changes fastest.
Arguments:
- initial: float32 [12, 32, 16, 512], P(None, 'gx', 'gy', 'gz'), may hold values from -4 to 4
- source: float32 [12, 32, 16, 512], P(None, 'gx', 'gy', 'gz'), may hold values from -6 to 6
- classes: int32 [32, 16, 512], P('gx', 'gy', 'gz'), may hold values from 0 to 15
- coupling: float32 [16], replicated, may hold values from 0.3 to 3
- owner: int32 [32, 16, 512], P('gx', 'gy', 'gz'), may hold values from 0 to 4095
- model: float32 [8, 8, 512], P('gx', 'gy', 'gz'), may hold values from -4 to 4
Outputs:
- fields: float32 [12, 32, 16, 512], P(None, 'gx', 'gy', 'gz')
- gradient: float32 [8, 8, 512], P('gx', 'gy', 'gz')
The draws below stay inside these ranges and needn't reach their ends.
Inputs may be any that keep to these rules, and one draw needn't show every extreme that they name: owner v of a cell at (x, y, z) names inversion cell v mod (1024) of the block of inversion cells with x index x // 8, y index y // 8 and depth index v // 1024.
All inputs are finite; a program needn't handle non-finite values.
Results may differ from the reference program's by a relative error of at most 0.00002.
Values sent between devices are 32-bit elements; how exact they have to be, the bound alone decides.
A program may use at most 64 MiB of HBM per device.

```python
import math
import jax
import jax.numpy as jnp

CX = 8
CY = 8
IX = 2
IY = 4
IZ = 128
CLASSES = 16
SWEEPS = 4
NX = 32
NY = 16
NZ = 512
MX = 8
MY = 8
MZ = 512
GROUP_CELLS = 4096


def plant(values, rng, smallest, largest):
    place = [jax.random.randint(jax.random.fold_in(rng, axis), (), 0, length) for axis, length in enumerate(values.shape)]
    main_axis = values.shape.index(max(values.shape))
    next_to = place[:main_axis] + [(place[main_axis] + 1) % values.shape[main_axis]] + place[main_axis + 1:]
    return values.at[tuple(place)].set(smallest).at[tuple(next_to)].set(largest)


def steps_of(rng, dims, shards, low, high):
    def one(position, parts):
        draws = jax.random.uniform(jax.random.fold_in(jax.random.fold_in(rng, 6), position), (parts,), jnp.float32, low / len(shards), high / len(shards))
        return jnp.repeat(jnp.exp(draws), dims[position] // parts).reshape((-1,) + (1,) * (len(dims) - position - 1))

    gain = one(*shards[0])
    for cut in shards[1:]:
        gain = gain * one(*cut)
    return gain


def noise(own_key, shape, width, limit, split=(), kind=jnp.bfloat16):
    entries = width * jax.random.normal(own_key, shape, jnp.float32)
    if split:
        entries = entries * steps_of(own_key, shape, split, -0.22, 0.18)
    return jnp.clip(entries, -limit, limit).astype(kind)


def setup_inputs(seed: int = 0) -> dict:
    streams_of = jax.random.split(jax.random.key(seed), 7)
    initial = noise(streams_of[0], (12, NX, NY, NZ), 0.5, 4.0, ((1, 4), (2, 2), (3, 4)), jnp.float32)
    source = noise(streams_of[1], (12, NX, NY, NZ), 1.0, 6.0, ((1, 4), (2, 2), (3, 4)), jnp.float32)
    classes = plant(jax.random.randint(streams_of[2], (NX, NY, NZ), 0, CLASSES), jax.random.fold_in(streams_of[2], 1), 0, CLASSES - 1).astype(jnp.int32)
    coupling = jnp.clip(jnp.exp(jax.random.uniform(streams_of[3], (CLASSES,), jnp.float32, math.log(0.3), math.log(3.0))), 0.3, 3.0)
    owner = plant(jax.random.randint(streams_of[4], (NX, NY, NZ), 0, GROUP_CELLS), jax.random.fold_in(streams_of[4], 1), 0, GROUP_CELLS - 1).astype(jnp.int32)
    model = noise(streams_of[5], (MX, MY, MZ), 0.5, 4.0, ((0, 4), (1, 2), (2, 4)), jnp.float32)
    return dict(initial=initial, source=source, classes=classes, coupling=coupling, owner=owner, model=model)


def neighbour_sum(padded):
    total = padded[..., 2:, 1:-1, 1:-1] + padded[..., :-2, 1:-1, 1:-1]
    total = total + padded[..., 1:-1, 2:, 1:-1] + padded[..., 1:-1, :-2, 1:-1]
    return total + padded[..., 1:-1, 1:-1, 2:] + padded[..., 1:-1, 1:-1, :-2]


def relax_sweep(center, padded, source_cells, coupling_cell):
    applied = 6.0 * center - neighbour_sum(padded)
    shape = (2, 3, 2) + center.shape[1:]
    centre_parts = center.reshape(shape)
    applied_parts = applied.reshape(shape)
    source_parts = source_cells.reshape(shape)
    resid_real = source_parts[:, :, 0] - (applied_parts[:, :, 0] - coupling_cell * centre_parts[:, :, 1])
    resid_imag = source_parts[:, :, 1] - (applied_parts[:, :, 1] + coupling_cell * centre_parts[:, :, 0])
    divisor = 36.0 + coupling_cell * coupling_cell
    step_real = (6.0 * resid_real + coupling_cell * resid_imag) / divisor
    step_imag = (6.0 * resid_imag - coupling_cell * resid_real) / divisor
    return center + 0.8 * jnp.stack([step_real, step_imag], axis=2).reshape(center.shape)


def reference(initial, source, classes, coupling, owner, model):
    coupling_cell = jnp.take(coupling, classes)
    fields = initial
    for sweep_index in range(SWEEPS):
        padded = jnp.pad(fields, ((0, 0), (1, 1), (1, 1), (1, 1)))
        fields = relax_sweep(fields, padded, source, coupling_cell)
    field_parts = fields.reshape((2, 3, 2) + fields.shape[1:])
    sens = coupling_cell * jnp.sum(field_parts[0, :, 0] * field_parts[1, :, 1] + field_parts[0, :, 1] * field_parts[1, :, 0], axis=0)
    inv_cells = IX * IY * IZ
    row_x = jnp.arange(NX, dtype=jnp.int32)[:, None, None]
    row_y = jnp.arange(NY, dtype=jnp.int32)[None, :, None]
    peer_index = owner // inv_cells
    local_index = owner % inv_cells
    inv_x = (row_x // CX) * IX + local_index // (IY * IZ)
    inv_y = (row_y // CY) * IY + (local_index // IZ) % IY
    inv_z = peer_index * IZ + local_index % IZ
    flat_index = ((inv_x * MY + inv_y) * MZ + inv_z).astype(jnp.int32)
    owned_sens = jax.ops.segment_sum(sens.reshape(-1), flat_index.reshape(-1), num_segments=MX * MY * MZ).reshape(MX, MY, MZ)
    gradient = owned_sens + 6.0 * model - neighbour_sum(jnp.pad(model, 1))
    return fields, gradient
```

```python
import functools

import jax
import jax.numpy as jnp
from jax import lax
from jax.experimental import pallas as pl
from jax.experimental.pallas import tpu as pltpu
from jax.sharding import PartitionSpec as P

SWEEPS = 4
MESH = pl.DeviceIdType.MESH
AXES = ("gx", "gy", "gz")
F32 = jnp.float32
BF16 = jnp.bfloat16


def kernel(
    sizes, init_hbm, src_hbm, cls_hbm, coup, own_hbm, mod_hbm, out, grad,
    init, src, cls, own, mod, f, part_next, const, ab, hx, hy, hz, sy, sz, hm, lo_hot, hi_hot, part, rs,
    load_sem, send_sem, recv_sem, msend, mrecv, rsend, rrecv,
):
    chans, nx, ny, nz = init.shape
    pairs = chans // 2
    per_vreg = chans * nx // 2
    pos = [lax.axis_index(a) for a in AXES]
    has = [(pos[i] > 0, pos[i] < sizes[i] - 1) for i in range(3)]
    n = sizes[2]
    peers = [lax.rem(pos[2] + d, n) for d in range(1, n)]
    ends = [[pos[i] - 1, pos[i] + 1] for i in range(3)]

    barrier = pltpu.get_barrier_semaphore()
    for i in range(2):
        for side in range(2):

            @pl.when(has[i][side])
            def _():
                pl.semaphore_signal(
                    barrier, inc=1, device_id={AXES[i]: ends[i][side]}, device_id_type=MESH
                )

    for d in range(1, n):
        pl.semaphore_signal(barrier, inc=1, device_id={"gz": peers[d - 1]}, device_id_type=MESH)
    greeted = n - 1
    for i in range(2):
        for side in range(2):
            greeted = greeted + has[i][side].astype(jnp.int32)

    loads = [
        pltpu.make_async_copy(a, b, load_sem.at[k])
        for k, (a, b) in enumerate(
            (
                (init_hbm, init), (mod_hbm, mod), (cls_hbm, cls), (src_hbm, src), (own_hbm, own),
            )
        )
    ]
    for load in loads:
        load.start()

    lane = lax.broadcasted_iota(jnp.int32, (ny, nz), 1)
    sub = lax.broadcasted_iota(jnp.int32, (ny, nz), 0)
    lane3 = lax.broadcasted_iota(jnp.int32, (nx, ny, nz), 2)
    sub3 = lax.broadcasted_iota(jnp.int32, (nx, ny, nz), 1)

    for i, halo in enumerate((hx, hy, hz)):
        for side in range(2):

            @pl.when(jnp.logical_not(has[i][side]))
            def _():
                halo[:, side] = jnp.zeros((SWEEPS,) + halo.shape[2:], F32)
                hm[2 * i + side] = jnp.zeros(hm.shape[1:], F32)

    def face(s, i, side):
        cells = init if s == 0 else f.at[s - 1]
        if i == 0:
            source = cells.at[:, 0 if side == 0 else nx - 1]
            halo = hx
        elif i == 1:
            source = sy.at[s, side]
            halo = hy
        else:
            source = sz.at[s]
            halo = hz
        return pltpu.make_async_remote_copy(
            src_ref=source,
            dst_ref=halo.at[s, 1 - side],
            send_sem=send_sem.at[s, 2 * i + side],
            recv_sem=recv_sem.at[s, 2 * i + 1 - side],
            device_id={AXES[i]: ends[i][side]},
            device_id_type=MESH,
        )

    def model_copy(i, side):
        return pltpu.make_async_remote_copy(
            src_ref=mod,
            dst_ref=hm.at[2 * i + 1 - side],
            send_sem=msend.at[2 * i + side],
            recv_sem=mrecv.at[2 * i + 1 - side],
            device_id={AXES[i]: ends[i][side]},
            device_id_type=MESH,
        )

    def start(make, i):
        for side in range(2):

            @pl.when(has[i][side])
            def _():
                make(i, side).start()

    def wait_recv(make, i):
        for side in range(2):

            @pl.when(has[i][side])
            def _():
                make(i, 1 - side).wait_recv()

    def wait_send(make, i):
        for side in range(2):

            @pl.when(has[i][side])
            def _():
                make(i, side).wait_send()

    def pack_y(cells, s):
        flat = cells.reshape(chans * nx * ny, nz)
        for c in range(chans):
            for side, row in ((0, 0), (1, ny - 1)):
                sy[s, side, c] = flat[pl.ds(c * nx * ny + row, nx, stride=ny), :]

    def pack_z(acc, value, j):
        return jnp.where((lane >> 1) == j, pltpu.roll(value, 2 * j + 1, 1), acc)

    loads[0].wait()
    pack_y(init, 0)
    for g in range(2):
        acc = jnp.zeros((ny, nz), F32)
        for j in range(per_vreg):
            c, x = divmod(g * per_vreg + j, nx)
            acc = pack_z(acc, init[c, x], j)
        sz[0, g] = acc

    pl.semaphore_wait(barrier, greeted)
    for i in range(3):
        start(functools.partial(face, 0), i)
    loads[1].wait()
    for i in range(3):
        start(model_copy, i)

    loads[2].wait()
    classes = cls[...]
    kappa = jnp.zeros(classes.shape, F32)
    for k in range(coup.shape[0]):
        kappa = jnp.where(classes == k, coup[k], kappa)
    scale = 0.8 / (36.0 + kappa * kappa)
    ab[0] = 6.0 * scale
    ab[1] = kappa * scale
    ab[2] = kappa

    def shifted(v):
        zero = jnp.zeros((1, ny, nz), F32)
        total = jnp.concatenate([zero, v[:-1]], 0) + jnp.concatenate([v[1:], zero], 0)
        total = total + jnp.where(sub3 == 0, 0.0, pltpu.roll(v, 1, 1))
        total = total + jnp.where(sub3 == ny - 1, 0.0, pltpu.roll(v, ny - 1, 1))
        total = total + jnp.where(lane3 == 0, 0.0, pltpu.roll(v, 1, 2))
        return total + jnp.where(lane3 == nz - 1, 0.0, pltpu.roll(v, nz - 1, 2))

    def local(s):
        cells = init if s == 0 else f.at[s - 1]

        def one(p, carry):
            a, b = ab[0], ab[1]
            fr, fi = cells[2 * p], cells[2 * p + 1]
            if s == 0:
                sr, si = src[2 * p], src[2 * p + 1]
                cr, ci = a * sr + b * si, a * si - b * sr
                const[2 * p] = cr
                const[2 * p + 1] = ci
            else:
                cr, ci = const[2 * p], const[2 * p + 1]
            tr, ti = shifted(fr), shifted(fi)
            part_next[2 * p] = cr + 0.2 * fr + (a * tr + b * ti)
            part_next[2 * p + 1] = ci + 0.2 * fi + (a * ti - b * tr)
            return carry

        lax.fori_loop(0, pairs, one, 0, unroll=True)

    def finish(s, planes, accs):
        results = []
        cells = out if s == SWEEPS - 1 else f.at[s]
        last = s == SWEEPS - 1
        merged = [
            jnp.where((lane & 1) == 0, hz[s, 0, g], pltpu.roll(hz[s, 1, g], nz - 2, 1))
            for g in range(2)
        ]
        edge = (lane == 0) | (lane == nz - 1)

        for g in range(2):

            def one(q, acc):
                for x in planes:
                    sums = []
                    for r in range(2):
                        c = g * (chans // 2) + 2 * q + r
                        j = (2 * q + r) * nx + x
                        low = jnp.broadcast_to(hy[s, 0, c, x : x + 1, :], (ny, nz))
                        high = jnp.broadcast_to(hy[s, 1, c, x : x + 1, :], (ny, nz))
                        h = jnp.where(sub == 0, low, jnp.where(sub == ny - 1, high, 0.0))
                        h = h + jnp.where(edge, pltpu.roll(merged[g], nz - 2 * j, 1), 0.0)
                        if x == 0:
                            h = h + hx[s, 0, c]
                        if x == nx - 1:
                            h = h + hx[s, 1, c]
                        sums.append(h)
                    a, b = ab[0, x], ab[1, x]
                    c = g * (chans // 2) + 2 * q
                    nr = part_next[c, x] + (a * sums[0] + b * sums[1])
                    ni = part_next[c + 1, x] + (a * sums[1] - b * sums[0])
                    cells[c, x] = nr
                    cells[c + 1, x] = ni
                    if not last:
                        acc = pack_z(acc, nr, 2 * q * nx + x)
                        acc = pack_z(acc, ni, (2 * q + 1) * nx + x)
                return acc

            first = jnp.zeros((ny, nz), F32) if accs is None else accs[g]
            results.append(lax.fori_loop(0, pairs // 2, one, first, unroll=True))
        return results

    groups = hi_hot.shape[0]

    def hots(x0, x1):
        rows = lax.broadcasted_iota(jnp.int32, (16, nz), 0)
        bands = [(rows + 16 * k).astype(F32).astype(BF16) for k in range(max(nz, groups) // 16)]
        yes, no = jnp.ones((16, nz), BF16), jnp.zeros((16, nz), BF16)

        def one(x, carry):
            for y in range(ny):
                v = own[x, y : y + 1, :]
                at = pl.ds(pl.multiple_of((x * ny + y) * nz, nz), nz)
                low = jnp.broadcast_to((v & (nz - 1)).astype(F32), (16, nz)).astype(BF16)
                high = jnp.broadcast_to((v >> 7).astype(F32), (16, nz)).astype(BF16)
                for k in range(nz // 16):
                    lo_hot[16 * k : 16 * k + 16, at] = jnp.where(bands[k] == low, yes, no)
                for k in range(groups // 16):
                    hi_hot[16 * k : 16 * k + 16, at] = jnp.where(bands[k] == high, yes, no)
            return carry

        lax.fori_loop(x0, x1, one, 0, unroll=True)

    loads[3].wait()
    loads[4].wait()
    for s in range(SWEEPS):
        local(s)
        hots(s * nx // SWEEPS, (s + 1) * nx // SWEEPS)
        for i in range(3):
            wait_recv(functools.partial(face, s), i)
        accs = finish(s, range(nx), None)
        if s < SWEEPS - 1:
            start(functools.partial(face, s + 1), 0)
            for g in range(2):
                sz[s + 1, g] = accs[g]
            start(functools.partial(face, s + 1), 2)
            pack_y(f.at[s], s + 1)
            start(functools.partial(face, s + 1), 1)

    def plane(x, total):
        sens = jnp.zeros((ny, nz), F32)
        for k in range(pairs // 2):
            fr, fi = out[2 * k, x], out[2 * k + 1, x]
            gr, gi = out[pairs + 2 * k, x], out[pairs + 2 * k + 1, x]
            sens = sens + (fr * gi + fi * gr)
        sens = ab[2, x] * sens
        s0 = sens.astype(BF16).astype(F32)
        rest = sens - s0
        s1 = rest.astype(BF16).astype(F32)
        s2 = rest - s1
        left = []
        for piece in (s0, s1, s2):
            row = jnp.concatenate(
                [jnp.broadcast_to(piece[y : y + 1, :], (groups, nz)) for y in range(ny)], 1
            ).astype(BF16)
            left.append(row)
        at = pl.ds(pl.multiple_of(x * ny * nz, nz), ny * nz)
        hi = hi_hot[:, at]
        lhs = jnp.concatenate([hi * row for row in left], 0)
        return total + lax.dot_general(
            lhs, lo_hot[:, at], (((1,), (1,)), ((), ())), preferred_element_type=F32
        )

    total = lax.fori_loop(0, nx, plane, jnp.zeros((3 * groups, nz), F32), unroll=True)
    part[...] = total[:groups] + total[groups : 2 * groups] + total[2 * groups :]

    rows = groups // n

    def rs_copy(d):
        return pltpu.make_async_remote_copy(
            src_ref=part.at[pl.ds(pl.multiple_of(peers[d - 1] * rows, rows), rows)],
            dst_ref=rs.at[d - 1],
            send_sem=rsend.at[d - 1],
            recv_sem=rrecv.at[d - 1],
            device_id={"gz": peers[d - 1]},
            device_id_type=MESH,
        )

    for d in range(1, n):
        rs_copy(d).start()

    for i in range(3):
        wait_recv(model_copy, i)
    m = mod[...]
    mz = m.shape[2]
    mlane = lax.broadcasted_iota(jnp.int32, m.shape, 2)
    total = jnp.concatenate([hm[0][-1:], m[:-1]], 0) + jnp.concatenate([m[1:], hm[1][:1]], 0)
    total = total + jnp.concatenate([hm[2][:, -1:], m[:, :-1]], 1)
    total = total + jnp.concatenate([m[:, 1:], hm[3][:, :1]], 1)
    total = total + pltpu.roll(jnp.where(mlane == mz - 1, hm[4], m), 1, 2)
    total = total + pltpu.roll(jnp.where(mlane == 0, hm[5], m), mz - 1, 2)
    smooth = 6.0 * m - total

    owned = part[pl.ds(pl.multiple_of(pos[2] * rows, rows), rows), :]
    for d in range(1, n):
        rs_copy(d).wait_recv()
    for d in range(1, n):
        owned = owned + rs[d - 1]
    my = m.shape[1]
    for k in range(m.shape[0]):
        grad[k] = owned[k * my : (k + 1) * my] + smooth[k]

    for s in range(SWEEPS):
        for i in range(3):
            wait_send(functools.partial(face, s), i)
    for i in range(3):
        wait_send(model_copy, i)
    for d in range(1, n):
        rs_copy(d).wait_send()


def flush(fields, grad, fields_hbm, grad_hbm, sem):
    copies = [
        pltpu.make_async_copy(fields, fields_hbm, sem.at[0]),
        pltpu.make_async_copy(grad, grad_hbm, sem.at[1]),
    ]
    for copy in copies:
        copy.start()
    for copy in copies:
        copy.wait()


def solution(mesh):
    sizes = tuple(mesh.shape[a] for a in AXES)

    def body(initial, source, classes, coupling, owner, model):
        chans, nx, ny, nz = initial.shape
        n = sizes[2]
        groups = n * model.size // nz
        dma = pltpu.SemaphoreType.DMA
        vmem = pl.BlockSpec(memory_space=pltpu.VMEM)
        hbm = pl.BlockSpec(memory_space=pltpu.HBM)
        results = pl.pallas_call(
            functools.partial(kernel, sizes),
            out_shape=(
                pltpu.VMEM(initial.shape, F32),
                pltpu.VMEM(model.shape, F32),
            ),
            in_specs=[hbm, hbm, hbm, pl.BlockSpec(memory_space=pltpu.SMEM), hbm, hbm],
            out_specs=(vmem, vmem),
            scratch_shapes=[
                pltpu.VMEM(initial.shape, F32),
                pltpu.VMEM(source.shape, F32),
                pltpu.VMEM(classes.shape, jnp.int32),
                pltpu.VMEM(owner.shape, jnp.int32),
                pltpu.VMEM(model.shape, F32),
                pltpu.VMEM((SWEEPS - 1, chans, nx, ny, nz), F32),
                pltpu.VMEM((chans, nx, ny, nz), F32),
                pltpu.VMEM((chans, nx, ny, nz), F32),
                pltpu.VMEM((3, nx, ny, nz), F32),
                pltpu.VMEM((SWEEPS, 2, chans, ny, nz), F32),
                pltpu.VMEM((SWEEPS, 2, chans, nx, nz), F32),
                pltpu.VMEM((SWEEPS, 2, 2, ny, nz), F32),
                pltpu.VMEM((SWEEPS, 2, chans, nx, nz), F32),
                pltpu.VMEM((SWEEPS, 2, ny, nz), F32),
                pltpu.VMEM((6,) + model.shape, F32),
                pltpu.VMEM((nz, nx * ny * nz), BF16),
                pltpu.VMEM((groups, nx * ny * nz), BF16),
                pltpu.VMEM((groups, nz), F32),
                pltpu.VMEM((n - 1, groups // n, nz), F32),
                dma((5,)),
                dma((SWEEPS, 6)),
                dma((SWEEPS, 6)),
                dma((6,)),
                dma((6,)),
                dma((n - 1,)),
                dma((n - 1,)),
            ],
            compiler_params=pltpu.CompilerParams(
                collective_id=0, has_side_effects=True, vmem_limit_bytes=60 * 1024 * 1024
            ),
        )(initial, source, classes, coupling, owner, model)
        return pl.pallas_call(
            flush,
            out_shape=(
                jax.ShapeDtypeStruct(initial.shape, F32),
                jax.ShapeDtypeStruct(model.shape, F32),
            ),
            in_specs=[vmem, vmem],
            out_specs=(hbm, hbm),
            scratch_shapes=[dma((2,))],
        )(*[pltpu.with_memory_space_constraint(r, pltpu.VMEM) for r in results])

    in_specs = (
        P(None, "gx", "gy", "gz"),
        P(None, "gx", "gy", "gz"),
        P("gx", "gy", "gz"),
        P(),
        P("gx", "gy", "gz"),
        P("gx", "gy", "gz"),
    )
    out_specs = (P(None, "gx", "gy", "gz"), P("gx", "gy", "gz"))
    return jax.shard_map(body, mesh=mesh, in_specs=in_specs, out_specs=out_specs, check_vma=False)
```

```python
import functools

import jax
import jax.numpy as jnp
from jax import lax
from jax.experimental import pallas as pl
from jax.experimental.pallas import tpu as pltpu
from jax.sharding import PartitionSpec as P

SWEEPS = 4
MESH = pl.DeviceIdType.MESH
AXES = ("gx", "gy", "gz")
F32 = jnp.float32
BF16 = jnp.bfloat16


def kernel(
    sizes, init_hbm, src_hbm, cls_hbm, coup_hbm, own_hbm, mod_hbm, out, grad,
    init, src, cls, coup, own, mod, f, part_next, const, ab, ycor, hx, hy, hz, sy, sz, hm, lo_hot, hi_hot, part, rs,
    load_sem, send_sem, recv_sem, msend, mrecv, rsend, rrecv,
):
    chans, nx, ny, nz = init.shape
    pairs = chans // 2
    half = chans // 2
    per_vreg = chans * nx // 2
    pos = [lax.axis_index(a) for a in AXES]
    has = [(pos[i] > 0, pos[i] < sizes[i] - 1) for i in range(3)]
    n = sizes[2]
    peers = [lax.rem(pos[2] + d, n) for d in range(1, n)]
    ends = [[pos[i] - 1, pos[i] + 1] for i in range(3)]

    barrier = pltpu.get_barrier_semaphore()
    for i in range(2):
        for side in range(2):

            @pl.when(has[i][side])
            def _():
                pl.semaphore_signal(
                    barrier, inc=1, device_id={AXES[i]: ends[i][side]}, device_id_type=MESH
                )

    for d in range(1, n):
        pl.semaphore_signal(barrier, inc=1, device_id={"gz": peers[d - 1]}, device_id_type=MESH)
    greeted = n - 1
    for i in range(2):
        for side in range(2):
            greeted = greeted + has[i][side].astype(jnp.int32)

    loads = [
        pltpu.make_async_copy(a, b, load_sem.at[k])
        for k, (a, b) in enumerate(
            (
                (init_hbm, init), (mod_hbm, mod), (cls_hbm, cls), (src_hbm, src), (own_hbm, own),
                (coup_hbm, coup),
            )
        )
    ]
    for load in loads:
        load.start()

    lane = lax.broadcasted_iota(jnp.int32, (ny, nz), 1)

    for i, halo in enumerate((hx, hy, hz)):
        for side in range(2):

            @pl.when(jnp.logical_not(has[i][side]))
            def _():
                halo[:, side] = jnp.zeros((SWEEPS,) + halo.shape[2:], F32)
                hm[2 * i + side] = jnp.zeros(hm.shape[1:], F32)

    def face(s, g, i, side):
        cells = init if s == 0 else f.at[s - 1]
        mine = pl.ds(g * half, half)
        if i == 0:
            source = cells.at[mine, 0 if side == 0 else nx - 1]
            halo = hx.at[s, 1 - side, mine]
        elif i == 1:
            source = sy.at[s, side, mine]
            halo = hy.at[s, 1 - side, mine]
        else:
            source = sz.at[s, g]
            halo = hz.at[s, 1 - side, g]
        return pltpu.make_async_remote_copy(
            src_ref=source,
            dst_ref=halo,
            send_sem=send_sem.at[s, g, 2 * i + side],
            recv_sem=recv_sem.at[s, g, 2 * i + 1 - side],
            device_id={AXES[i]: ends[i][side]},
            device_id_type=MESH,
        )

    def model_copy(i, side):
        return pltpu.make_async_remote_copy(
            src_ref=mod,
            dst_ref=hm.at[2 * i + 1 - side],
            send_sem=msend.at[2 * i + side],
            recv_sem=mrecv.at[2 * i + 1 - side],
            device_id={AXES[i]: ends[i][side]},
            device_id_type=MESH,
        )

    def start(make, i):
        for side in range(2):

            @pl.when(has[i][side])
            def _():
                make(i, side).start()

    def wait_recv(make, i):
        for side in range(2):

            @pl.when(has[i][side])
            def _():
                make(i, 1 - side).wait_recv()

    def wait_send(make, i):
        for side in range(2):

            @pl.when(has[i][side])
            def _():
                make(i, side).wait_send()

    def pack_y(cells, s, g):
        flat = cells.reshape(chans * nx * ny, nz)
        for c in range(g * half, g * half + half):
            for side, row in ((0, 0), (1, ny - 1)):
                sy[s, side, c] = flat[pl.ds(c * nx * ny + row, nx, stride=ny), :]

    def pack_z(acc, value, j):
        return jnp.where((lane >> 1) == j, pltpu.roll(value, 2 * j + 1, 1), acc)

    loads[0].wait()
    for g in range(2):
        pack_y(init, 0, g)
        acc = jnp.zeros((ny, nz), F32)
        for j in range(per_vreg):
            c, x = divmod(g * per_vreg + j, nx)
            acc = pack_z(acc, init[c, x], j)
        sz[0, g] = acc

    pl.semaphore_wait(barrier, greeted)
    for g in range(2):
        for i in (1, 2, 0):
            start(functools.partial(face, 0, g), i)
    loads[1].wait()
    for i in range(3):
        start(model_copy, i)

    loads[2].wait()
    loads[5].wait()
    classes = cls[...]
    kappa = jnp.zeros(classes.shape, F32)
    for k in range(coup.shape[0]):
        kappa = jnp.where(classes == k, coup[k], kappa)
    scale = 0.8 / (36.0 + kappa * kappa)
    ab[0] = 6.0 * scale
    ab[1] = kappa * scale
    ab[2] = kappa

    def shifted(v):
        zero = jnp.zeros((1, ny, nz), F32)
        total = jnp.concatenate([zero, v[:-1]], 0) + jnp.concatenate([v[1:], zero], 0)
        total = total + (pltpu.roll(v, 1, 1) + pltpu.roll(v, ny - 1, 1))
        return total + (pltpu.roll(v, 1, 2) + pltpu.roll(v, nz - 1, 2))

    def local(s, g):
        cells = init if s == 0 else f.at[s - 1]

        def one(p, carry):
            a, b = ab[0], ab[1]
            fr, fi = cells[2 * p], cells[2 * p + 1]
            if s == 0:
                sr, si = src[2 * p], src[2 * p + 1]
                cr, ci = a * sr + b * si, a * si - b * sr
                const[2 * p] = cr
                const[2 * p + 1] = ci
            else:
                cr, ci = const[2 * p], const[2 * p + 1]
            tr, ti = shifted(fr), shifted(fi)
            part_next[2 * p] = cr + 0.2 * fr + (a * tr + b * ti)
            part_next[2 * p + 1] = ci + 0.2 * fi + (a * ti - b * tr)
            return carry

        lax.fori_loop(g * pairs // 2, (g + 1) * pairs // 2, one, 0, unroll=True)

    ycor[...] = jnp.zeros(ycor.shape, F32)

    def finish(s, g):
        cells = out if s == SWEEPS - 1 else f.at[s]
        last = s == SWEEPS - 1
        own_z = sz[s, g]
        merged = jnp.where(
            (lane & 1) == 0, hz[s, 0, g] - own_z, pltpu.roll(hz[s, 1, g] - own_z, nz - 2, 1)
        )
        edge = (lane == 0) | (lane == nz - 1)
        rows = ycor.reshape(chans * nx * ny, nz)
        for c in range(g * half, g * half + half):
            for side, row in ((0, 0), (1, ny - 1)):
                rows[pl.ds(c * nx * ny + row, nx, stride=ny), :] = (
                    hy[s, side, c] - sy[s, 1 - side, c]
                )

        def one(q, acc):
            c = g * half + 2 * q
            for x in range(nx):
                sums = []
                for r in range(2):
                    j = (2 * q + r) * nx + x
                    h = ycor[c + r, x] + jnp.where(edge, pltpu.roll(merged, nz - 2 * j, 1), 0.0)
                    if x == 0:
                        h = h + hx[s, 0, c + r]
                    if x == nx - 1:
                        h = h + hx[s, 1, c + r]
                    sums.append(h)
                a, b = ab[0, x], ab[1, x]
                nr = part_next[c, x] + (a * sums[0] + b * sums[1])
                ni = part_next[c + 1, x] + (a * sums[1] - b * sums[0])
                cells[c, x] = nr
                cells[c + 1, x] = ni
                if not last:
                    acc = pack_z(acc, nr, 2 * q * nx + x)
                    acc = pack_z(acc, ni, (2 * q + 1) * nx + x)
            return acc

        return lax.fori_loop(0, pairs // 2, one, jnp.zeros((ny, nz), F32), unroll=True)

    groups = hi_hot.shape[0]

    def hots(x0, x1):
        rows = lax.broadcasted_iota(jnp.int32, (16, nz), 0)
        bands = [(rows + 16 * k).astype(F32).astype(BF16) for k in range(max(nz, groups) // 16)]
        yes, no = jnp.ones((16, nz), BF16), jnp.zeros((16, nz), BF16)

        def one(x, carry):
            for y in range(ny):
                v = own[x, y : y + 1, :]
                at = pl.ds(pl.multiple_of((x * ny + y) * nz, nz), nz)
                low = jnp.broadcast_to((v & (nz - 1)).astype(F32), (16, nz)).astype(BF16)
                high = jnp.broadcast_to((v >> 7).astype(F32), (16, nz)).astype(BF16)
                for k in range(nz // 16):
                    lo_hot[16 * k : 16 * k + 16, at] = jnp.where(bands[k] == low, yes, no)
                for k in range(groups // 16):
                    hi_hot[16 * k : 16 * k + 16, at] = jnp.where(bands[k] == high, yes, no)
            return carry

        lax.fori_loop(x0, x1, one, 0, unroll=True)

    loads[3].wait()
    loads[4].wait()
    for g in range(2):
        local(0, g)
    hots(0, nx // SWEEPS)
    for s in range(SWEEPS):
        for g in range(2):
            for i in (0, 2, 1):
                wait_recv(functools.partial(face, s, g), i)
            packed = finish(s, g)
            if s < SWEEPS - 1:
                sz[s + 1, g] = packed
                pack_y(f.at[s], s + 1, g)
                for i in (1, 2, 0):
                    start(functools.partial(face, s + 1, g), i)
                local(s + 1, g)
        if s < SWEEPS - 1:
            hots((s + 1) * nx // SWEEPS, (s + 2) * nx // SWEEPS)

    def plane(x, total):
        sens = jnp.zeros((ny, nz), F32)
        for k in range(pairs // 2):
            fr, fi = out[2 * k, x], out[2 * k + 1, x]
            gr, gi = out[pairs + 2 * k, x], out[pairs + 2 * k + 1, x]
            sens = sens + (fr * gi + fi * gr)
        sens = ab[2, x] * sens
        s0 = sens.astype(BF16).astype(F32)
        rest = sens - s0
        s1 = rest.astype(BF16).astype(F32)
        s2 = rest - s1
        left = []
        for piece in (s0, s1, s2):
            row = jnp.concatenate(
                [jnp.broadcast_to(piece[y : y + 1, :], (groups, nz)) for y in range(ny)], 1
            ).astype(BF16)
            left.append(row)
        at = pl.ds(pl.multiple_of(x * ny * nz, nz), ny * nz)
        hi = hi_hot[:, at]
        lhs = jnp.concatenate([hi * row for row in left], 0)
        return total + lax.dot_general(
            lhs, lo_hot[:, at], (((1,), (1,)), ((), ())), preferred_element_type=F32
        )

    total = lax.fori_loop(0, nx, plane, jnp.zeros((3 * groups, nz), F32), unroll=True)
    part[...] = total[:groups] + total[groups : 2 * groups] + total[2 * groups :]

    rows = groups // n

    def rs_copy(d):
        return pltpu.make_async_remote_copy(
            src_ref=part.at[pl.ds(pl.multiple_of(peers[d - 1] * rows, rows), rows)],
            dst_ref=rs.at[d - 1],
            send_sem=rsend.at[d - 1],
            recv_sem=rrecv.at[d - 1],
            device_id={"gz": peers[d - 1]},
            device_id_type=MESH,
        )

    for d in range(1, n):
        rs_copy(d).start()

    for i in range(3):
        wait_recv(model_copy, i)
    m = mod[...]
    mz = m.shape[2]
    mlane = lax.broadcasted_iota(jnp.int32, m.shape, 2)
    total = jnp.concatenate([hm[0][-1:], m[:-1]], 0) + jnp.concatenate([m[1:], hm[1][:1]], 0)
    total = total + jnp.concatenate([hm[2][:, -1:], m[:, :-1]], 1)
    total = total + jnp.concatenate([m[:, 1:], hm[3][:, :1]], 1)
    total = total + pltpu.roll(jnp.where(mlane == mz - 1, hm[4], m), 1, 2)
    total = total + pltpu.roll(jnp.where(mlane == 0, hm[5], m), mz - 1, 2)
    smooth = 6.0 * m - total

    owned = part[pl.ds(pl.multiple_of(pos[2] * rows, rows), rows), :]
    for d in range(1, n):
        rs_copy(d).wait_recv()
    for d in range(1, n):
        owned = owned + rs[d - 1]
    my = m.shape[1]
    for k in range(m.shape[0]):
        grad[k] = owned[k * my : (k + 1) * my] + smooth[k]

    for s in range(SWEEPS):
        for g in range(2):
            for i in range(3):
                wait_send(functools.partial(face, s, g), i)
    for i in range(3):
        wait_send(model_copy, i)
    for d in range(1, n):
        rs_copy(d).wait_send()


def flush(fields, grad, fields_hbm, grad_hbm, sem):
    copies = [
        pltpu.make_async_copy(fields, fields_hbm, sem.at[0]),
        pltpu.make_async_copy(grad, grad_hbm, sem.at[1]),
    ]
    for copy in copies:
        copy.start()
    for copy in copies:
        copy.wait()


def solution(mesh):
    sizes = tuple(mesh.shape[a] for a in AXES)

    def body(initial, source, classes, coupling, owner, model):
        chans, nx, ny, nz = initial.shape
        n = sizes[2]
        groups = n * model.size // nz
        dma = pltpu.SemaphoreType.DMA
        vmem = pl.BlockSpec(memory_space=pltpu.VMEM)
        hbm = pl.BlockSpec(memory_space=pltpu.HBM)
        results = pl.pallas_call(
            functools.partial(kernel, sizes),
            out_shape=(
                pltpu.VMEM(initial.shape, F32),
                pltpu.VMEM(model.shape, F32),
            ),
            in_specs=[hbm] * 6,
            out_specs=(vmem, vmem),
            scratch_shapes=[
                pltpu.VMEM(initial.shape, F32),
                pltpu.VMEM(source.shape, F32),
                pltpu.VMEM(classes.shape, jnp.int32),
                pltpu.SMEM(coupling.shape, F32),
                pltpu.VMEM(owner.shape, jnp.int32),
                pltpu.VMEM(model.shape, F32),
                pltpu.VMEM((SWEEPS - 1, chans, nx, ny, nz), F32),
                pltpu.VMEM((chans, nx, ny, nz), F32),
                pltpu.VMEM((chans, nx, ny, nz), F32),
                pltpu.VMEM((3, nx, ny, nz), F32),
                pltpu.VMEM((chans, nx, ny, nz), F32),
                pltpu.VMEM((SWEEPS, 2, chans, ny, nz), F32),
                pltpu.VMEM((SWEEPS, 2, chans, nx, nz), F32),
                pltpu.VMEM((SWEEPS, 2, 2, ny, nz), F32),
                pltpu.VMEM((SWEEPS, 2, chans, nx, nz), F32),
                pltpu.VMEM((SWEEPS, 2, ny, nz), F32),
                pltpu.VMEM((6,) + model.shape, F32),
                pltpu.VMEM((nz, nx * ny * nz), BF16),
                pltpu.VMEM((groups, nx * ny * nz), BF16),
                pltpu.VMEM((groups, nz), F32),
                pltpu.VMEM((n - 1, groups // n, nz), F32),
                dma((6,)),
                dma((SWEEPS, 2, 6)),
                dma((SWEEPS, 2, 6)),
                dma((6,)),
                dma((6,)),
                dma((n - 1,)),
                dma((n - 1,)),
            ],
            compiler_params=pltpu.CompilerParams(
                collective_id=0, has_side_effects=True, vmem_limit_bytes=60 * 1024 * 1024
            ),
        )(initial, source, classes, coupling, owner, model)
        return pl.pallas_call(
            flush,
            out_shape=(
                jax.ShapeDtypeStruct(initial.shape, F32),
                jax.ShapeDtypeStruct(model.shape, F32),
            ),
            in_specs=[vmem, vmem],
            out_specs=(hbm, hbm),
            scratch_shapes=[dma((2,))],
        )(*[pltpu.with_memory_space_constraint(r, pltpu.VMEM) for r in results])

    in_specs = (
        P(None, "gx", "gy", "gz"),
        P(None, "gx", "gy", "gz"),
        P("gx", "gy", "gz"),
        P(),
        P("gx", "gy", "gz"),
        P("gx", "gy", "gz"),
    )
    out_specs = (P(None, "gx", "gy", "gz"), P("gx", "gy", "gz"))
    return jax.shard_map(body, mesh=mesh, in_specs=in_specs, out_specs=out_specs, check_vma=False)
```

```python
import functools

import jax
import jax.numpy as jnp
from jax import lax
from jax.experimental import pallas as pl
from jax.experimental.pallas import tpu as pltpu
from jax.sharding import PartitionSpec as P

SWEEPS = 4
MESH = pl.DeviceIdType.MESH
AXES = ("gx", "gy", "gz")
F32 = jnp.float32
BF16 = jnp.bfloat16


def kernel(
    sizes, init_hbm, src_hbm, cls_hbm, coup_hbm, own_hbm, mod_hbm, out, grad,
    init, src, cls, coup, own, mod, f, part_next, const, kap, ycor,
    hx, hy, hy2, hz, hxy, hxz, hyz, hcx, hcy, hcz, sy, sy2, sz, sxy, scy, scz,
    hm, lo_hot, hi_hot, part, rs,
    load_sem, send_sem, recv_sem, esend, erecv, csend, crecv, msend, mrecv, rsend, rrecv,
):
    chans, nx, ny, nz = init.shape
    pairs = chans // 2
    half = chans // 2
    per_vreg = chans * nx // 2
    pos = [lax.axis_index(a) for a in AXES]
    has = [(pos[i] > 0, pos[i] < sizes[i] - 1) for i in range(3)]
    n = sizes[2]
    peers = [lax.rem(pos[2] + d, n) for d in range(1, n)]
    ends = [[pos[i] - 1, pos[i] + 1] for i in range(3)]
    lines = [
        (m, i, j, si, sj)
        for m, (i, j) in enumerate(((0, 1), (0, 2), (1, 2)))
        for si in range(2)
        for sj in range(2)
    ]

    barrier = pltpu.get_barrier_semaphore()
    for i in range(2):
        for side in range(2):

            @pl.when(has[i][side])
            def _():
                pl.semaphore_signal(
                    barrier, inc=1, device_id={AXES[i]: ends[i][side]}, device_id_type=MESH
                )

    for d in range(1, n):
        pl.semaphore_signal(barrier, inc=1, device_id={"gz": peers[d - 1]}, device_id_type=MESH)

    def met(i, j, si, sj):
        return jnp.logical_and(has[i][si], has[j][sj])

    for m, i, j, si, sj in lines:

        @pl.when(met(i, j, si, sj))
        def _():
            pl.semaphore_signal(
                barrier,
                inc=1,
                device_id={AXES[i]: ends[i][si], AXES[j]: ends[j][sj]},
                device_id_type=MESH,
            )

    greeted = n - 1
    for i in range(2):
        for side in range(2):
            greeted = greeted + has[i][side].astype(jnp.int32)
    for m, i, j, si, sj in lines:
        greeted = greeted + met(i, j, si, sj).astype(jnp.int32)

    loads = [
        pltpu.make_async_copy(a, b, load_sem.at[k])
        for k, (a, b) in enumerate(
            (
                (init_hbm, init), (mod_hbm, mod), (cls_hbm, cls), (src_hbm, src), (own_hbm, own),
                (coup_hbm, coup),
            )
        )
    ]
    for load in loads:
        load.start()

    lane = lax.broadcasted_iota(jnp.int32, (ny, nz), 1)
    sub = lax.broadcasted_iota(jnp.int32, (ny, nz), 0)
    even = (lane & 1) == 0
    shift3 = jnp.where(even, lane, lane - 3)
    xlane = (lane >> 1) % nx
    real = ((lane // (2 * nx)) & 1) == 0

    for i, halo in enumerate((hx, hy, hz)):
        for side in range(2):

            @pl.when(jnp.logical_not(has[i][side]))
            def _():
                halo[:, side] = jnp.zeros(halo.shape[:1] + halo.shape[2:], F32)
                hm[2 * i + side] = jnp.zeros(hm.shape[1:], F32)

    held = (hxy, hxz, hyz)
    for m, i, j, si, sj in lines:

        @pl.when(jnp.logical_not(met(i, j, si, sj)))
        def _():
            line = held[m]
            line[:, 2 * si + sj] = jnp.zeros(line.shape[:1] + line.shape[2:], F32)

    def face(e, g, i, side):
        s = 2 * e
        cells = init if e == 0 else f.at[s - 1]
        mine = pl.ds(g * half, half)
        axis = i
        if i == 0:
            source = cells.at[mine, pl.ds(0 if side == 0 else nx - 2, 2)]
            halo = hx.at[s, 1 - side, mine]
        elif i == 1:
            source = sy.at[s, side, mine]
            halo = hy.at[s, 1 - side, mine]
        elif i == 2:
            source = sz.at[s, g]
            halo = hz.at[s, 1 - side, g]
        else:
            axis = 1
            source = sy2.at[e, side, mine]
            halo = hy2.at[e, 1 - side, mine]
        return pltpu.make_async_remote_copy(
            src_ref=source,
            dst_ref=halo,
            send_sem=send_sem.at[e, g, 2 * i + side],
            recv_sem=recv_sem.at[e, g, 2 * i + 1 - side],
            device_id={AXES[axis]: ends[axis][side]},
            device_id_type=MESH,
        )

    def line_copy(e, m, i, j, si, sj):
        s = 2 * e
        source = (sxy.at[e, 2 * si + sj], sz.at[s, :, 0], sz.at[s, :, pl.ds(0, 2)])[m]
        there = 2 * (1 - si) + 1 - sj
        return pltpu.make_async_remote_copy(
            src_ref=source,
            dst_ref=held[m].at[e, there],
            send_sem=esend.at[e, 4 * m + 2 * si + sj],
            recv_sem=erecv.at[e, 4 * m + there],
            device_id={AXES[i]: ends[i][si], AXES[j]: ends[j][sj]},
            device_id_type=MESH,
        )

    def start_lines(e):
        for m, i, j, si, sj in lines:

            @pl.when(met(i, j, si, sj))
            def _():
                line_copy(e, m, i, j, si, sj).start()

    def wait_lines(e):
        for m, i, j, si, sj in lines:

            @pl.when(met(i, j, si, sj))
            def _():
                line_copy(e, m, i, j, 1 - si, 1 - sj).wait_recv()

    def wait_lines_sent(e):
        for m, i, j, si, sj in lines:

            @pl.when(met(i, j, si, sj))
            def _():
                line_copy(e, m, i, j, si, sj).wait_send()

    def const_copy(i, side):
        if i == 0:
            source, halo = const.at[:, 0 if side == 0 else nx - 1], hcx
        elif i == 1:
            source, halo = scy.at[side], hcy
        else:
            source, halo = scz, hcz
        return pltpu.make_async_remote_copy(
            src_ref=source,
            dst_ref=halo.at[1 - side],
            send_sem=csend.at[2 * i + side],
            recv_sem=crecv.at[2 * i + 1 - side],
            device_id={AXES[i]: ends[i][side]},
            device_id_type=MESH,
        )

    def model_copy(i, side):
        return pltpu.make_async_remote_copy(
            src_ref=mod,
            dst_ref=hm.at[2 * i + 1 - side],
            send_sem=msend.at[2 * i + side],
            recv_sem=mrecv.at[2 * i + 1 - side],
            device_id={AXES[i]: ends[i][side]},
            device_id_type=MESH,
        )

    def start(make, i):
        for side in range(2):

            @pl.when(has[i % 2 if i == 3 else i][side])
            def _():
                make(i, side).start()

    def wait_recv(make, i):
        for side in range(2):

            @pl.when(has[i % 2 if i == 3 else i][side])
            def _():
                make(i, 1 - side).wait_recv()

    def wait_send(make, i):
        for side in range(2):

            @pl.when(has[i % 2 if i == 3 else i][side])
            def _():
                make(i, side).wait_send()

    def rows_of(cells, into, channels, rows):
        flat = cells.reshape(cells.shape[0] * nx * ny, nz)
        for c in channels:
            for side, row in enumerate(rows):
                into[side, c] = flat[pl.ds(c * nx * ny + row, nx, stride=ny), :]

    def channels_of(g):
        return range(g * half, g * half + half)

    def pack_z(acc, value, j):
        return jnp.where((lane >> 1) == j, pltpu.roll(value, 2 * j + 1, 1), acc)

    def pack_z2(acc, value, j):
        return jnp.where(shift3 == 2 * j, pltpu.roll(value, 2 * j + 2, 1), acc)

    def pack_rows(cells, s, g):
        rows_of(cells, sy.at[s], channels_of(g), (0, ny - 1))

    def pack_exchange(cells, e, g):
        s = 2 * e
        pack_rows(cells, s, g)
        rows_of(cells, sy2.at[e], channels_of(g), (1, ny - 2))
        acc = jnp.zeros((nx, nz), F32)
        for k in range(half):
            for side in range(2):
                acc = pack_z(acc, sy[s, side, g * half + k], 2 * k + side)
        sz[s, g, 1] = acc

    def pack_corners(e):
        for side in range(2):
            flat = sy.at[2 * e, side].reshape(chans * nx, nz)
            for end, x in enumerate((0, nx - 1)):
                sxy[e, 2 * end + side, 0:chans] = flat[pl.ds(x, chans, stride=nx), :]

    def send_exchange(e, g):
        for i in (1, 2, 0):
            start(functools.partial(face, e, g), i)

    def send_rest(e):
        for g in range(2):
            start(functools.partial(face, e, g), 3)
        start_lines(e)

    loads[0].wait()
    for g in range(2):
        pack_exchange(init, 0, g)
        acc = jnp.zeros((ny, nz), F32)
        acc2 = jnp.zeros((ny, nz), F32)
        for j in range(per_vreg):
            c, x = divmod(g * per_vreg + j, nx)
            cell = init[c, x]
            acc = pack_z(acc, cell, j)
            acc2 = pack_z2(acc2, cell, j)
        sz[0, g, 0] = acc
        sz[0, g, 2] = acc2
    pack_corners(0)

    pl.semaphore_wait(barrier, greeted)
    for g in range(2):
        send_exchange(0, g)
    send_rest(0)
    loads[1].wait()
    for i in range(3):
        start(model_copy, i)

    loads[2].wait()
    loads[5].wait()
    classes = cls[...]
    kappa = jnp.zeros(classes.shape, F32)
    for k in range(coup.shape[0]):
        kappa = jnp.where(classes == k, coup[k], kappa)
    scale = 0.8 / (36.0 + kappa * kappa)
    const[chans] = 6.0 * scale
    const[chans + 1] = kappa * scale
    kap[...] = kappa

    def shifted(v):
        zero = jnp.zeros((1, ny, nz), F32)
        total = jnp.concatenate([zero, v[:-1]], 0) + jnp.concatenate([v[1:], zero], 0)
        total = total + (pltpu.roll(v, 1, 1) + pltpu.roll(v, ny - 1, 1))
        return total + (pltpu.roll(v, 1, 2) + pltpu.roll(v, nz - 1, 2))

    def local(s, g):
        cells = init if s == 0 else f.at[s - 1]

        def one(p, carry):
            a, b = const[chans], const[chans + 1]
            fr, fi = cells[2 * p], cells[2 * p + 1]
            if s == 0:
                sr, si = src[2 * p], src[2 * p + 1]
                cr, ci = a * sr + b * si, a * si - b * sr
                const[2 * p] = cr
                const[2 * p + 1] = ci
            else:
                cr, ci = const[2 * p], const[2 * p + 1]
            tr, ti = shifted(fr), shifted(fi)
            part_next[2 * p] = cr + 0.2 * fr + (a * tr + b * ti)
            part_next[2 * p + 1] = ci + 0.2 * fi + (a * ti - b * tr)
            return carry

        lax.fori_loop(g * pairs // 2, (g + 1) * pairs // 2, one, 0, unroll=True)

    ycor[...] = jnp.zeros(ycor.shape, F32)

    def merge(low, high):
        return jnp.where(even, low, pltpu.roll(high, nz - 2, 1))

    def finish(s, g):
        cells = out if s == SWEEPS - 1 else f.at[s]
        last = s == SWEEPS - 1
        deep = s % 2 == 1 and not last
        own_z = sz[s, g, 0]
        merged = merge(hz[s, 0, g, 0] - own_z, hz[s, 1, g, 0] - own_z)
        edge = (lane == 0) | (lane == nz - 1)
        rows = ycor.reshape(chans * nx * ny, nz)
        for c in channels_of(g):
            for side, row in ((0, 0), (1, ny - 1)):
                rows[pl.ds(c * nx * ny + row, nx, stride=ny), :] = (
                    hy[s, side, c] - sy[s, 1 - side, c]
                )

        def one(q, accs):
            acc, acc2 = accs
            c = g * half + 2 * q
            for x in range(nx):
                sums = []
                for r in range(2):
                    j = (2 * q + r) * nx + x
                    h = ycor[c + r, x] + jnp.where(edge, pltpu.roll(merged, nz - 2 * j, 1), 0.0)
                    if x == 0:
                        h = h + hx[s, 0, c + r, 1]
                    if x == nx - 1:
                        h = h + hx[s, 1, c + r, 0]
                    sums.append(h)
                a, b = const[chans, x], const[chans + 1, x]
                nr = part_next[c, x] + (a * sums[0] + b * sums[1])
                ni = part_next[c + 1, x] + (a * sums[1] - b * sums[0])
                cells[c, x] = nr
                cells[c + 1, x] = ni
                for r, value in enumerate((nr, ni)):
                    j = (2 * q + r) * nx + x
                    if not last:
                        acc = pack_z(acc, value, j)
                    if deep:
                        acc2 = pack_z2(acc2, value, j)
            return acc, acc2

        zero = jnp.zeros((ny, nz), F32)
        acc, acc2 = lax.fori_loop(0, pairs // 2, one, (zero, zero), unroll=True)
        if not last:
            sz[s + 1, g, 0] = acc
        if deep:
            sz[s + 1, g, 2] = acc2

    def stepped(fixed, field, total, a, b):
        tr, ti = total
        return (
            fixed[0] + 0.2 * field[0] + (a * tr + b * ti),
            fixed[1] + 0.2 * field[1] + (a * ti - b * tr),
        )

    def around(field, low, high, ends_z):
        count = field.shape[0]
        total = jnp.where(sub == 0, low, pltpu.roll(field, 1, 0))
        total = total + jnp.where(sub == count - 1, high, pltpu.roll(field, count - 1, 0))
        total = total + jnp.where(lane == 0, ends_z, pltpu.roll(field, 1, 1))
        return total + jnp.where(lane == nz - 1, ends_z, pltpu.roll(field, nz - 1, 1))

    def spread(row, count):
        return jnp.broadcast_to(row, (count, nz))

    def kept(i, side, value):
        return jnp.where(has[i][side], value, 0.0)

    def outer(e):
        s = 2 * e
        cells = init if e == 0 else f.at[s - 1]
        both = [(g, side) for g in range(2) for side in range(2)]

        for g, side in both:
            v = hz[s, side, g, 0]
            second = hz[s, side, g, 2]
            if side == 1:
                second = pltpu.roll(second, nz - 2, 1)
            mine = pltpu.roll(sz[s, g, 0], nz - 1 if side == 0 else 1, 1)
            low = spread(hyz[e, side, g, 0, ny - 1 : ny, :], ny)
            high = spread(hyz[e, 2 + side, g, 0, 0:1, :], ny)
            t = second + mine
            t = t + jnp.where(sub == 0, low, pltpu.roll(v, 1, 0))
            t = t + jnp.where(sub == ny - 1, high, pltpu.roll(v, ny - 1, 0))
            over = 2 * (nx - 1)
            t = t + jnp.where(
                xlane == 0, pltpu.roll(hxz[e, side, g], nz - over, 1), pltpu.roll(v, 2, 1)
            )
            t = t + jnp.where(
                xlane == nx - 1,
                pltpu.roll(hxz[e, 2 + side, g], over, 1),
                pltpu.roll(v, nz - 2, 1),
            )
            other = jnp.where(real, pltpu.roll(t, nz - 2 * nx, 1), -pltpu.roll(t, 2 * nx, 1))
            new = hcz[side, g] + 0.2 * v + (hcz[side, 2] * t + hcz[side, 3] * other)
            hz[s + 1, side, g, 0] = kept(2, side, new)

        for g, side in both:
            ends_z = merge(hyz[e, 2 * side, g, 1], hyz[e, 2 * side + 1, g, 1])
            a, b = hcy[side, chans], hcy[side, chans + 1]
            for q in range(half // 2):
                c = g * half + 2 * q
                fields, totals = [], []
                for r in range(2):
                    j = 2 * (2 * q + r) + 1 - side
                    v = hy[s, side, c + r]
                    low = spread(hxy[e, side, c + r : c + r + 1, :], nx)
                    high = spread(hxy[e, 2 + side, c + r : c + r + 1, :], nx)
                    t = around(v, low, high, pltpu.roll(ends_z, (nz - 2 * j) % nz, 1))
                    fields.append(v)
                    totals.append(t + hy2[e, side, c + r] + sy[s, side, c + r])
                nr, ni = stepped((hcy[side, c], hcy[side, c + 1]), fields, totals, a, b)
                hy[s + 1, side, c] = kept(1, side, nr)
                hy[s + 1, side, c + 1] = kept(1, side, ni)

        for g, side in both:
            one, two = (1, 0) if side == 0 else (0, 1)
            x = 0 if side == 0 else nx - 1
            ends_z = merge(hxz[e, 2 * side, g], hxz[e, 2 * side + 1, g])
            a, b = hcx[side, chans], hcx[side, chans + 1]
            for q in range(half // 2):
                c = g * half + 2 * q
                fields, totals = [], []
                for r in range(2):
                    j = (2 * q + r) * nx + (nx - 1 - x)
                    v = hx[s, side, c + r, one]
                    low = spread(hxy[e, 2 * side, c + r : c + r + 1, :], ny)
                    high = spread(hxy[e, 2 * side + 1, c + r : c + r + 1, :], ny)
                    t = around(v, low, high, pltpu.roll(ends_z, (nz - 2 * j) % nz, 1))
                    fields.append(v)
                    totals.append(t + hx[s, side, c + r, two] + cells[c + r, x])
                nr, ni = stepped((hcx[side, c], hcx[side, c + 1]), fields, totals, a, b)
                hx[s + 1, side, c, one] = kept(0, side, nr)
                hx[s + 1, side, c + 1, one] = kept(0, side, ni)

    groups = hi_hot.shape[0]

    def hots(x0, x1):
        rows = lax.broadcasted_iota(jnp.int32, (16, nz), 0)
        bands = [(rows + 16 * k).astype(F32).astype(BF16) for k in range(max(nz, groups) // 16)]
        yes, no = jnp.ones((16, nz), BF16), jnp.zeros((16, nz), BF16)

        def one(x, carry):
            for y in range(ny):
                v = own[x, y : y + 1, :]
                at = pl.ds(pl.multiple_of((x * ny + y) * nz, nz), nz)
                low = jnp.broadcast_to((v & (nz - 1)).astype(F32), (16, nz)).astype(BF16)
                high = jnp.broadcast_to((v >> 7).astype(F32), (16, nz)).astype(BF16)
                for k in range(nz // 16):
                    lo_hot[16 * k : 16 * k + 16, at] = jnp.where(bands[k] == low, yes, no)
                for k in range(groups // 16):
                    hi_hot[16 * k : 16 * k + 16, at] = jnp.where(bands[k] == high, yes, no)
            return carry

        lax.fori_loop(x0, x1, one, 0, unroll=True)

    loads[3].wait()
    loads[4].wait()
    for g in range(2):
        local(0, g)
    rows_of(const, scy, range(chans + 2), (0, ny - 1))
    for g in range(4):
        acc = jnp.zeros((ny, nz), F32)
        for j in range(per_vreg if g < 2 else nx):
            c, x = divmod(g * per_vreg + j, nx) if g < 2 else (chans + g - 2, j)
            acc = pack_z(acc, const[c, x], j)
        block = 2 * nx
        while g >= 2 and block < nz:
            acc = acc + pltpu.roll(acc, block, 1)
            block *= 2
        scz[g] = acc
    for i in (1, 2, 0):
        start(const_copy, i)
    hots(0, nx // 2)
    for e in range(SWEEPS // 2):
        s = 2 * e
        for g in range(2):
            for i in (0, 2, 1):
                wait_recv(functools.partial(face, e, g), i)
            finish(s, g)
            pack_rows(f.at[s], s + 1, g)
            local(s + 1, g)
        if e == 0:
            for i in range(3):
                wait_recv(const_copy, i)
        wait_lines(e)
        for g in range(2):
            wait_recv(functools.partial(face, e, g), 3)
        outer(e)
        for g in range(2):
            finish(s + 1, g)
            if s + 2 < SWEEPS:
                pack_exchange(f.at[s + 1], e + 1, g)
                send_exchange(e + 1, g)
        if s + 2 < SWEEPS:
            pack_corners(e + 1)
            send_rest(e + 1)
            for g in range(2):
                local(s + 2, g)
            if e == 0:
                hots(nx // 2, nx)

    def plane(x, total):
        sens = jnp.zeros((ny, nz), F32)
        for k in range(pairs // 2):
            fr, fi = out[2 * k, x], out[2 * k + 1, x]
            gr, gi = out[pairs + 2 * k, x], out[pairs + 2 * k + 1, x]
            sens = sens + (fr * gi + fi * gr)
        sens = kap[x] * sens
        s0 = sens.astype(BF16).astype(F32)
        rest = sens - s0
        s1 = rest.astype(BF16).astype(F32)
        s2 = rest - s1
        left = []
        for piece in (s0, s1, s2):
            row = jnp.concatenate(
                [jnp.broadcast_to(piece[y : y + 1, :], (groups, nz)) for y in range(ny)], 1
            ).astype(BF16)
            left.append(row)
        at = pl.ds(pl.multiple_of(x * ny * nz, nz), ny * nz)
        hi = hi_hot[:, at]
        lhs = jnp.concatenate([hi * row for row in left], 0)
        return total + lax.dot_general(
            lhs, lo_hot[:, at], (((1,), (1,)), ((), ())), preferred_element_type=F32
        )

    total = lax.fori_loop(0, nx, plane, jnp.zeros((3 * groups, nz), F32), unroll=True)
    part[...] = total[:groups] + total[groups : 2 * groups] + total[2 * groups :]

    rows = groups // n

    def rs_copy(d):
        return pltpu.make_async_remote_copy(
            src_ref=part.at[pl.ds(pl.multiple_of(peers[d - 1] * rows, rows), rows)],
            dst_ref=rs.at[d - 1],
            send_sem=rsend.at[d - 1],
            recv_sem=rrecv.at[d - 1],
            device_id={"gz": peers[d - 1]},
            device_id_type=MESH,
        )

    for d in range(1, n):
        rs_copy(d).start()

    for i in range(3):
        wait_recv(model_copy, i)
    m = mod[...]
    mz = m.shape[2]
    mlane = lax.broadcasted_iota(jnp.int32, m.shape, 2)
    total = jnp.concatenate([hm[0][-1:], m[:-1]], 0) + jnp.concatenate([m[1:], hm[1][:1]], 0)
    total = total + jnp.concatenate([hm[2][:, -1:], m[:, :-1]], 1)
    total = total + jnp.concatenate([m[:, 1:], hm[3][:, :1]], 1)
    total = total + pltpu.roll(jnp.where(mlane == mz - 1, hm[4], m), 1, 2)
    total = total + pltpu.roll(jnp.where(mlane == 0, hm[5], m), mz - 1, 2)
    smooth = 6.0 * m - total

    for e in range(SWEEPS // 2):
        for g in range(2):
            for i in range(4):
                wait_send(functools.partial(face, e, g), i)
        wait_lines_sent(e)
    for i in range(3):
        wait_send(const_copy, i)
    for i in range(3):
        wait_send(model_copy, i)

    owned = part[pl.ds(pl.multiple_of(pos[2] * rows, rows), rows), :]
    for d in range(1, n):
        rs_copy(d).wait_recv()
    for d in range(1, n):
        owned = owned + rs[d - 1]
    my = m.shape[1]
    for k in range(m.shape[0]):
        grad[k] = owned[k * my : (k + 1) * my] + smooth[k]

    for d in range(1, n):
        rs_copy(d).wait_send()


def flush(fields, grad, fields_hbm, grad_hbm, sem):
    copies = [
        pltpu.make_async_copy(fields, fields_hbm, sem.at[0]),
        pltpu.make_async_copy(grad, grad_hbm, sem.at[1]),
    ]
    for copy in copies:
        copy.start()
    for copy in copies:
        copy.wait()


def solution(mesh):
    sizes = tuple(mesh.shape[a] for a in AXES)

    def body(initial, source, classes, coupling, owner, model):
        chans, nx, ny, nz = initial.shape
        n = sizes[2]
        groups = n * model.size // nz
        dma = pltpu.SemaphoreType.DMA
        vmem = pl.BlockSpec(memory_space=pltpu.VMEM)
        hbm = pl.BlockSpec(memory_space=pltpu.HBM)
        results = pl.pallas_call(
            functools.partial(kernel, sizes),
            out_shape=(
                pltpu.VMEM(initial.shape, F32),
                pltpu.VMEM(model.shape, F32),
            ),
            in_specs=[hbm] * 6,
            out_specs=(vmem, vmem),
            scratch_shapes=[
                pltpu.VMEM(initial.shape, F32),
                pltpu.VMEM(source.shape, F32),
                pltpu.VMEM(classes.shape, jnp.int32),
                pltpu.SMEM(coupling.shape, F32),
                pltpu.VMEM(owner.shape, jnp.int32),
                pltpu.VMEM(model.shape, F32),
                pltpu.VMEM((SWEEPS - 1, chans, nx, ny, nz), F32),
                pltpu.VMEM((chans, nx, ny, nz), F32),
                pltpu.VMEM((chans + 2, nx, ny, nz), F32),
                pltpu.VMEM((nx, ny, nz), F32),
                pltpu.VMEM((chans, nx, ny, nz), F32),
                pltpu.VMEM((SWEEPS, 2, chans, 2, ny, nz), F32),
                pltpu.VMEM((SWEEPS, 2, chans, nx, nz), F32),
                pltpu.VMEM((SWEEPS // 2, 2, chans, nx, nz), F32),
                pltpu.VMEM((SWEEPS, 2, 2, 3, ny, nz), F32),
                pltpu.VMEM((SWEEPS // 2, 4, 16, nz), F32),
                pltpu.VMEM((SWEEPS // 2, 4, 2, ny, nz), F32),
                pltpu.VMEM((SWEEPS // 2, 4, 2, 2, ny, nz), F32),
                pltpu.VMEM((2, chans + 2, ny, nz), F32),
                pltpu.VMEM((2, chans + 2, nx, nz), F32),
                pltpu.VMEM((2, 4, ny, nz), F32),
                pltpu.VMEM((SWEEPS, 2, chans, nx, nz), F32),
                pltpu.VMEM((SWEEPS // 2, 2, chans, nx, nz), F32),
                pltpu.VMEM((SWEEPS, 2, 3, ny, nz), F32),
                pltpu.VMEM((SWEEPS // 2, 4, 16, nz), F32),
                pltpu.VMEM((2, chans + 2, nx, nz), F32),
                pltpu.VMEM((4, ny, nz), F32),
                pltpu.VMEM((6,) + model.shape, F32),
                pltpu.VMEM((nz, nx * ny * nz), BF16),
                pltpu.VMEM((groups, nx * ny * nz), BF16),
                pltpu.VMEM((groups, nz), F32),
                pltpu.VMEM((n - 1, groups // n, nz), F32),
                dma((6,)),
                dma((SWEEPS // 2, 2, 8)),
                dma((SWEEPS // 2, 2, 8)),
                dma((SWEEPS // 2, 12)),
                dma((SWEEPS // 2, 12)),
                dma((6,)),
                dma((6,)),
                dma((6,)),
                dma((6,)),
                dma((n - 1,)),
                dma((n - 1,)),
            ],
            compiler_params=pltpu.CompilerParams(
                collective_id=0, has_side_effects=True, vmem_limit_bytes=60 * 1024 * 1024
            ),
        )(initial, source, classes, coupling, owner, model)
        return pl.pallas_call(
            flush,
            out_shape=(
                jax.ShapeDtypeStruct(initial.shape, F32),
                jax.ShapeDtypeStruct(model.shape, F32),
            ),
            in_specs=[vmem, vmem],
            out_specs=(hbm, hbm),
            scratch_shapes=[dma((2,))],
        )(*[pltpu.with_memory_space_constraint(r, pltpu.VMEM) for r in results])

    in_specs = (
        P(None, "gx", "gy", "gz"),
        P(None, "gx", "gy", "gz"),
        P("gx", "gy", "gz"),
        P(),
        P("gx", "gy", "gz"),
        P("gx", "gy", "gz"),
    )
    out_specs = (P(None, "gx", "gy", "gz"), P("gx", "gy", "gz"))
    return jax.shard_map(body, mesh=mesh, in_specs=in_specs, out_specs=out_specs, check_vma=False)
```

```python
import functools

import jax
import jax.numpy as jnp
from jax import lax
from jax.experimental import pallas as pl
from jax.experimental.pallas import tpu as pltpu
from jax.sharding import PartitionSpec as P

SWEEPS = 4
MESH = pl.DeviceIdType.MESH
AXES = ("gx", "gy", "gz")
F32 = jnp.float32
BF16 = jnp.bfloat16


def kernel(
    sizes, init_hbm, src_hbm, cls_hbm, coup_hbm, own_hbm, mod_hbm, out, grad,
    init, src, cls, coup, own, mod, f, part_next, const, kap, ycor,
    hx, hy, hz, hxy, hxz, hyz, hcx, hcy, hcz, sy, sz, sxy, syz, scy, scz,
    hm, lo_hot, hi_hot, part, rs,
    load_sem, send_sem, recv_sem, esend, erecv, csend, crecv, msend, mrecv, rsend, rrecv,
):
    chans, nx, ny, nz = init.shape
    pairs = chans // 2
    half = chans // 2
    per_vreg = chans * nx // 2
    pos = [lax.axis_index(a) for a in AXES]
    has = [(pos[i] > 0, pos[i] < sizes[i] - 1) for i in range(3)]
    n = sizes[2]
    peers = [lax.rem(pos[2] + d, n) for d in range(1, n)]
    ends = [[pos[i] - 1, pos[i] + 1] for i in range(3)]
    lines = [
        (m, i, j, si, sj)
        for m, (i, j) in enumerate(((0, 1), (0, 2), (1, 2)))
        for si in range(2)
        for sj in range(2)
    ]

    barrier = pltpu.get_barrier_semaphore()
    for i in range(2):
        for side in range(2):

            @pl.when(has[i][side])
            def _():
                pl.semaphore_signal(
                    barrier, inc=1, device_id={AXES[i]: ends[i][side]}, device_id_type=MESH
                )

    for d in range(1, n):
        pl.semaphore_signal(barrier, inc=1, device_id={"gz": peers[d - 1]}, device_id_type=MESH)

    def met(i, j, si, sj):
        return jnp.logical_and(has[i][si], has[j][sj])

    for m, i, j, si, sj in lines:

        @pl.when(met(i, j, si, sj))
        def _():
            pl.semaphore_signal(
                barrier,
                inc=1,
                device_id={AXES[i]: ends[i][si], AXES[j]: ends[j][sj]},
                device_id_type=MESH,
            )

    greeted = n - 1
    for i in range(2):
        for side in range(2):
            greeted = greeted + has[i][side].astype(jnp.int32)
    for m, i, j, si, sj in lines:
        greeted = greeted + met(i, j, si, sj).astype(jnp.int32)

    loads = [
        pltpu.make_async_copy(a, b, load_sem.at[k])
        for k, (a, b) in enumerate(
            (
                (init_hbm, init), (mod_hbm, mod), (cls_hbm, cls), (src_hbm, src), (own_hbm, own),
                (coup_hbm, coup),
            )
        )
    ]
    for load in loads:
        load.start()

    lane = lax.broadcasted_iota(jnp.int32, (ny, nz), 1)
    sub = lax.broadcasted_iota(jnp.int32, (ny, nz), 0)
    even = (lane & 1) == 0
    shift3 = jnp.where(even, lane, lane - 3)
    xlane = (lane >> 1) % nx
    real = ((lane // (2 * nx)) & 1) == 0

    for i, halo in enumerate((hx, hy, hz)):
        for side in range(2):

            @pl.when(jnp.logical_not(has[i][side]))
            def _():
                halo[:, side] = jnp.zeros(halo.shape[:1] + halo.shape[2:], F32)
                hm[2 * i + side] = jnp.zeros(hm.shape[1:], F32)

    held = (hxy, hxz, hyz)
    for m, i, j, si, sj in lines:

        @pl.when(jnp.logical_not(met(i, j, si, sj)))
        def _():
            line = held[m]
            line[:, 2 * si + sj] = jnp.zeros(line.shape[:1] + line.shape[2:], F32)

    def face(e, i, side):
        s = 2 * e
        cells = init if e == 0 else f.at[s - 1]
        axis = min(i, 2)
        if i == 0:
            source = cells.at[:, pl.ds(0 if side == 0 else nx - 2, 2)]
            halo = hx.at[s, 1 - side]
        elif i == 2:
            source = sz.at[s]
            halo = hz.at[s, 1 - side]
        else:
            axis = 1
            mine = pl.ds(0 if i == 1 else half, half)
            source = sy.at[s, side, :, mine]
            halo = hy.at[s, 1 - side, :, mine]
        return pltpu.make_async_remote_copy(
            src_ref=source,
            dst_ref=halo,
            send_sem=send_sem.at[e, 2 * i + side],
            recv_sem=recv_sem.at[e, 2 * i + 1 - side],
            device_id={AXES[axis]: ends[axis][side]},
            device_id_type=MESH,
        )

    def line_copy(e, m, i, j, si, sj):
        s = 2 * e
        source = (sxy.at[e, 2 * si + sj], sz.at[s, :, 0], syz.at[e])[m]
        there = 2 * (1 - si) + 1 - sj
        return pltpu.make_async_remote_copy(
            src_ref=source,
            dst_ref=held[m].at[e, there],
            send_sem=esend.at[e, 4 * m + 2 * si + sj],
            recv_sem=erecv.at[e, 4 * m + there],
            device_id={AXES[i]: ends[i][si], AXES[j]: ends[j][sj]},
            device_id_type=MESH,
        )

    def start_lines(e):
        for m, i, j, si, sj in lines:

            @pl.when(met(i, j, si, sj))
            def _():
                line_copy(e, m, i, j, si, sj).start()

    def wait_lines(e):
        for m, i, j, si, sj in lines:

            @pl.when(met(i, j, si, sj))
            def _():
                line_copy(e, m, i, j, 1 - si, 1 - sj).wait_recv()

    def wait_lines_sent(e):
        for m, i, j, si, sj in lines:

            @pl.when(met(i, j, si, sj))
            def _():
                line_copy(e, m, i, j, si, sj).wait_send()

    def const_copy(i, side):
        if i == 0:
            source, halo = const.at[:, 0 if side == 0 else nx - 1], hcx
        elif i == 1:
            source, halo = scy.at[side], hcy
        else:
            source, halo = scz, hcz
        return pltpu.make_async_remote_copy(
            src_ref=source,
            dst_ref=halo.at[1 - side],
            send_sem=csend.at[2 * i + side],
            recv_sem=crecv.at[2 * i + 1 - side],
            device_id={AXES[i]: ends[i][side]},
            device_id_type=MESH,
        )

    def model_copy(i, side):
        return pltpu.make_async_remote_copy(
            src_ref=mod,
            dst_ref=hm.at[2 * i + 1 - side],
            send_sem=msend.at[2 * i + side],
            recv_sem=mrecv.at[2 * i + 1 - side],
            device_id={AXES[i]: ends[i][side]},
            device_id_type=MESH,
        )

    def start(make, i):
        for side in range(2):

            @pl.when(has[i % 2 if i == 3 else i][side])
            def _():
                make(i, side).start()

    def wait_recv(make, i):
        for side in range(2):

            @pl.when(has[i % 2 if i == 3 else i][side])
            def _():
                make(i, 1 - side).wait_recv()

    def wait_send(make, i):
        for side in range(2):

            @pl.when(has[i % 2 if i == 3 else i][side])
            def _():
                make(i, side).wait_send()

    def channels_of(g):
        return range(g * half, g * half + half)

    def pack_z(acc, value, j):
        return jnp.where((lane >> 1) == j, pltpu.roll(value, 2 * j + 1, 1), acc)

    def pack_z2(acc, value, j):
        return jnp.where(shift3 == 2 * j, pltpu.roll(value, 2 * j + 2, 1), acc)

    def pack_rows(cells, s, g, layer=0):
        flat = cells.reshape(chans * nx * ny, nz)
        for c in channels_of(g):
            for side, row in enumerate((layer, ny - 1 - layer)):
                sy[s, side, layer, c] = flat[pl.ds(c * nx * ny + row, nx, stride=ny), :]

    def pack_lines(e):
        s = 2 * e
        acc = jnp.zeros((nx, nz), F32)
        for c in range(chans):
            for side in range(2):
                acc = pack_z(acc, sy[s, side, 0, c], 2 * c + side)
        syz[e, 0] = acc
        for g in range(2):
            for side, row in enumerate((0, ny - 1)):
                at = 2 * side + g
                syz[e, 1, at : at + 1, :] = sz[s, g, 0, row : row + 1, :]
        for side in range(2):
            flat = sy.at[s, side, 0].reshape(chans * nx, nz)
            for end, x in enumerate((0, nx - 1)):
                sxy[e, 2 * end + side, 0:chans] = flat[pl.ds(x, chans, stride=nx), :]

    loads[0].wait()
    for g in range(2):
        pack_rows(init, 0, g)
        pack_rows(init, 0, g, 1)
        acc = jnp.zeros((ny, nz), F32)
        acc2 = jnp.zeros((ny, nz), F32)
        for j in range(per_vreg):
            c, x = divmod(g * per_vreg + j, nx)
            cell = init[c, x]
            acc = pack_z(acc, cell, j)
            acc2 = pack_z2(acc2, cell, j)
        sz[0, g, 0] = acc
        sz[0, g, 1] = acc2
    pack_lines(0)

    pl.semaphore_wait(barrier, greeted)
    for i in (1, 3, 2, 0):
        start(functools.partial(face, 0), i)
    start_lines(0)
    loads[1].wait()
    for i in range(3):
        start(model_copy, i)

    loads[2].wait()
    loads[5].wait()
    classes = cls[...]
    kappa = jnp.zeros(classes.shape, F32)
    for k in range(coup.shape[0]):
        kappa = jnp.where(classes == k, coup[k], kappa)
    scale = 0.8 / (36.0 + kappa * kappa)
    const[chans] = 6.0 * scale
    const[chans + 1] = kappa * scale
    kap[...] = kappa

    def shifted(v):
        zero = jnp.zeros((1, ny, nz), F32)
        total = jnp.concatenate([zero, v[:-1]], 0) + jnp.concatenate([v[1:], zero], 0)
        total = total + (pltpu.roll(v, 1, 1) + pltpu.roll(v, ny - 1, 1))
        return total + (pltpu.roll(v, 1, 2) + pltpu.roll(v, nz - 1, 2))

    def local(s, g):
        cells = init if s == 0 else f.at[s - 1]

        def one(p, carry):
            a, b = const[chans], const[chans + 1]
            fr, fi = cells[2 * p], cells[2 * p + 1]
            if s == 0:
                sr, si = src[2 * p], src[2 * p + 1]
                cr, ci = a * sr + b * si, a * si - b * sr
                const[2 * p] = cr
                const[2 * p + 1] = ci
            else:
                cr, ci = const[2 * p], const[2 * p + 1]
            tr, ti = shifted(fr), shifted(fi)
            part_next[2 * p] = cr + 0.2 * fr + (a * tr + b * ti)
            part_next[2 * p + 1] = ci + 0.2 * fi + (a * ti - b * tr)
            return carry

        lax.fori_loop(g * pairs // 2, (g + 1) * pairs // 2, one, 0, unroll=True)

    ycor[...] = jnp.zeros(ycor.shape, F32)

    def merge(low, high):
        return jnp.where(even, low, pltpu.roll(high, nz - 2, 1))

    def finish(s, g):
        cells = out if s == SWEEPS - 1 else f.at[s]
        last = s == SWEEPS - 1
        deep = s % 2 == 1 and not last
        own_z = sz[s, g, 0]
        merged = merge(hz[s, 0, g, 0] - own_z, hz[s, 1, g, 0] - own_z)
        edge = (lane == 0) | (lane == nz - 1)
        rows = ycor.reshape(chans * nx * ny, nz)
        for c in channels_of(g):
            for side, row in ((0, 0), (1, ny - 1)):
                rows[pl.ds(c * nx * ny + row, nx, stride=ny), :] = (
                    hy[s, side, 0, c] - sy[s, 1 - side, 0, c]
                )

        def one(q, accs):
            acc, acc2 = accs
            c = g * half + 2 * q
            for x in range(nx):
                sums = []
                for r in range(2):
                    j = (2 * q + r) * nx + x
                    h = ycor[c + r, x] + jnp.where(edge, pltpu.roll(merged, nz - 2 * j, 1), 0.0)
                    if x == 0:
                        h = h + hx[s, 0, c + r, 1]
                    if x == nx - 1:
                        h = h + hx[s, 1, c + r, 0]
                    sums.append(h)
                a, b = const[chans, x], const[chans + 1, x]
                nr = part_next[c, x] + (a * sums[0] + b * sums[1])
                ni = part_next[c + 1, x] + (a * sums[1] - b * sums[0])
                cells[c, x] = nr
                cells[c + 1, x] = ni
                for r, value in enumerate((nr, ni)):
                    j = (2 * q + r) * nx + x
                    if not last:
                        acc = pack_z(acc, value, j)
                    if deep:
                        acc2 = pack_z2(acc2, value, j)
            return acc, acc2

        zero = jnp.zeros((ny, nz), F32)
        acc, acc2 = lax.fori_loop(0, pairs // 2, one, (zero, zero), unroll=True)
        if not last:
            sz[s + 1, g, 0] = acc
        if deep:
            sz[s + 1, g, 1] = acc2

    def stepped(fixed, field, total, a, b):
        tr, ti = total
        return (
            fixed[0] + 0.2 * field[0] + (a * tr + b * ti),
            fixed[1] + 0.2 * field[1] + (a * ti - b * tr),
        )

    def around(field, low, high, ends_z):
        count = field.shape[0]
        total = jnp.where(sub == 0, low, pltpu.roll(field, 1, 0))
        total = total + jnp.where(sub == count - 1, high, pltpu.roll(field, count - 1, 0))
        total = total + jnp.where(lane == 0, ends_z, pltpu.roll(field, 1, 1))
        return total + jnp.where(lane == nz - 1, ends_z, pltpu.roll(field, nz - 1, 1))

    def spread(row, count):
        return jnp.broadcast_to(row, (count, nz))

    def kept(i, side, value):
        return jnp.where(has[i][side], value, 0.0)

    def outer(e, only):
        s = 2 * e
        cells = init if e == 0 else f.at[s - 1]
        both = [(g, side) for g in only for side in range(2)]

        for g, side in both:
            v = hz[s, side, g, 0]
            second = hz[s, side, g, 1]
            if side == 1:
                second = pltpu.roll(second, nz - 2, 1)
            mine = pltpu.roll(sz[s, g, 0], nz - 1 if side == 0 else 1, 1)
            low = spread(hyz[e, side, 1, 2 + g : 3 + g, :], ny)
            high = spread(hyz[e, 2 + side, 1, g : g + 1, :], ny)
            t = second + mine
            t = t + jnp.where(sub == 0, low, pltpu.roll(v, 1, 0))
            t = t + jnp.where(sub == ny - 1, high, pltpu.roll(v, ny - 1, 0))
            over = 2 * (nx - 1)
            t = t + jnp.where(
                xlane == 0, pltpu.roll(hxz[e, side, g], nz - over, 1), pltpu.roll(v, 2, 1)
            )
            t = t + jnp.where(
                xlane == nx - 1,
                pltpu.roll(hxz[e, 2 + side, g], over, 1),
                pltpu.roll(v, nz - 2, 1),
            )
            other = jnp.where(real, pltpu.roll(t, nz - 2 * nx, 1), -pltpu.roll(t, 2 * nx, 1))
            new = hcz[side, g] + 0.2 * v + (hcz[side, 2] * t + hcz[side, 3] * other)
            hz[s + 1, side, g, 0] = kept(2, side, new)

        for g, side in both:
            ends_z = merge(hyz[e, 2 * side, 0], hyz[e, 2 * side + 1, 0])
            a, b = hcy[side, chans], hcy[side, chans + 1]
            for q in range(half // 2):
                c = g * half + 2 * q
                fields, totals = [], []
                for r in range(2):
                    j = 2 * (c + r) + 1 - side
                    v = hy[s, side, 0, c + r]
                    low = spread(hxy[e, side, c + r : c + r + 1, :], nx)
                    high = spread(hxy[e, 2 + side, c + r : c + r + 1, :], nx)
                    t = around(v, low, high, pltpu.roll(ends_z, (nz - 2 * j) % nz, 1))
                    fields.append(v)
                    totals.append(t + hy[s, side, 1, c + r] + sy[s, side, 0, c + r])
                nr, ni = stepped((hcy[side, c], hcy[side, c + 1]), fields, totals, a, b)
                hy[s + 1, side, 0, c] = kept(1, side, nr)
                hy[s + 1, side, 0, c + 1] = kept(1, side, ni)

        for g, side in both:
            one, two = (1, 0) if side == 0 else (0, 1)
            x = 0 if side == 0 else nx - 1
            ends_z = merge(hxz[e, 2 * side, g], hxz[e, 2 * side + 1, g])
            a, b = hcx[side, chans], hcx[side, chans + 1]
            for q in range(half // 2):
                c = g * half + 2 * q
                fields, totals = [], []
                for r in range(2):
                    j = (2 * q + r) * nx + (nx - 1 - x)
                    v = hx[s, side, c + r, one]
                    low = spread(hxy[e, 2 * side, c + r : c + r + 1, :], ny)
                    high = spread(hxy[e, 2 * side + 1, c + r : c + r + 1, :], ny)
                    t = around(v, low, high, pltpu.roll(ends_z, (nz - 2 * j) % nz, 1))
                    fields.append(v)
                    totals.append(t + hx[s, side, c + r, two] + cells[c + r, x])
                nr, ni = stepped((hcx[side, c], hcx[side, c + 1]), fields, totals, a, b)
                hx[s + 1, side, c, one] = kept(0, side, nr)
                hx[s + 1, side, c + 1, one] = kept(0, side, ni)

    groups = hi_hot.shape[0]

    def hots(x0, x1):
        rows = lax.broadcasted_iota(jnp.int32, (16, nz), 0)
        bands = [(rows + 16 * k).astype(F32).astype(BF16) for k in range(max(nz, groups) // 16)]
        yes, no = jnp.ones((16, nz), BF16), jnp.zeros((16, nz), BF16)

        def one(x, carry):
            for y in range(ny):
                v = own[x, y : y + 1, :]
                at = pl.ds(pl.multiple_of((x * ny + y) * nz, nz), nz)
                low = jnp.broadcast_to((v & (nz - 1)).astype(F32), (16, nz)).astype(BF16)
                high = jnp.broadcast_to((v >> 7).astype(F32), (16, nz)).astype(BF16)
                for k in range(nz // 16):
                    lo_hot[16 * k : 16 * k + 16, at] = jnp.where(bands[k] == low, yes, no)
                for k in range(groups // 16):
                    hi_hot[16 * k : 16 * k + 16, at] = jnp.where(bands[k] == high, yes, no)
            return carry

        lax.fori_loop(x0, x1, one, 0, unroll=True)

    loads[3].wait()
    loads[4].wait()
    for g in range(2):
        local(0, g)
    flat = const.reshape((chans + 2) * nx * ny, nz)
    for c in range(chans + 2):
        for side, row in enumerate((0, ny - 1)):
            scy[side, c] = flat[pl.ds(c * nx * ny + row, nx, stride=ny), :]
    for g in range(4):
        acc = jnp.zeros((ny, nz), F32)
        for j in range(per_vreg if g < 2 else nx):
            c, x = divmod(g * per_vreg + j, nx) if g < 2 else (chans + g - 2, j)
            acc = pack_z(acc, const[c, x], j)
        block = 2 * nx
        while g >= 2 and block < nz:
            acc = acc + pltpu.roll(acc, block, 1)
            block *= 2
        scz[g] = acc
    for i in (1, 2, 0):
        start(const_copy, i)
    hots(0, nx // 2)
    for e in range(SWEEPS // 2):
        s = 2 * e
        for g in range(2):
            for i in (1, 0, 2) if g == 0 else (3,):
                wait_recv(functools.partial(face, e), i)
            finish(s, g)
            pack_rows(f.at[s], s + 1, g)
            local(s + 1, g)
        if e == 0:
            for i in range(3):
                wait_recv(const_copy, i)
        wait_lines(e)
        for g in range(2):
            outer(e, (g,))
            finish(s + 1, g)
            if s + 2 < SWEEPS:
                pack_rows(f.at[s + 1], s + 2, g)
                pack_rows(f.at[s + 1], s + 2, g, 1)
                start(functools.partial(face, e + 1), 1 + 2 * g)
        if s + 2 < SWEEPS:
            for i in (2, 0):
                start(functools.partial(face, e + 1), i)
            pack_lines(e + 1)
            start_lines(e + 1)
            for g in range(2):
                local(s + 2, g)
            if e == 0:
                hots(nx // 2, nx)

    def plane(x, total):
        sens = jnp.zeros((ny, nz), F32)
        for k in range(pairs // 2):
            fr, fi = out[2 * k, x], out[2 * k + 1, x]
            gr, gi = out[pairs + 2 * k, x], out[pairs + 2 * k + 1, x]
            sens = sens + (fr * gi + fi * gr)
        sens = kap[x] * sens
        s0 = sens.astype(BF16).astype(F32)
        rest = sens - s0
        s1 = rest.astype(BF16).astype(F32)
        s2 = rest - s1
        left = []
        for piece in (s0, s1, s2):
            row = jnp.concatenate(
                [jnp.broadcast_to(piece[y : y + 1, :], (groups, nz)) for y in range(ny)], 1
            ).astype(BF16)
            left.append(row)
        at = pl.ds(pl.multiple_of(x * ny * nz, nz), ny * nz)
        hi = hi_hot[:, at]
        lhs = jnp.concatenate([hi * row for row in left], 0)
        return total + lax.dot_general(
            lhs, lo_hot[:, at], (((1,), (1,)), ((), ())), preferred_element_type=F32
        )

    total = lax.fori_loop(0, nx, plane, jnp.zeros((3 * groups, nz), F32), unroll=True)
    part[...] = total[:groups] + total[groups : 2 * groups] + total[2 * groups :]

    rows = groups // n

    def rs_copy(d):
        return pltpu.make_async_remote_copy(
            src_ref=part.at[pl.ds(pl.multiple_of(peers[d - 1] * rows, rows), rows)],
            dst_ref=rs.at[d - 1],
            send_sem=rsend.at[d - 1],
            recv_sem=rrecv.at[d - 1],
            device_id={"gz": peers[d - 1]},
            device_id_type=MESH,
        )

    for d in range(1, n):
        rs_copy(d).start()

    for i in range(3):
        wait_recv(model_copy, i)
    m = mod[...]
    mz = m.shape[2]
    mlane = lax.broadcasted_iota(jnp.int32, m.shape, 2)
    total = jnp.concatenate([hm[0][-1:], m[:-1]], 0) + jnp.concatenate([m[1:], hm[1][:1]], 0)
    total = total + jnp.concatenate([hm[2][:, -1:], m[:, :-1]], 1)
    total = total + jnp.concatenate([m[:, 1:], hm[3][:, :1]], 1)
    total = total + pltpu.roll(jnp.where(mlane == mz - 1, hm[4], m), 1, 2)
    total = total + pltpu.roll(jnp.where(mlane == 0, hm[5], m), mz - 1, 2)
    smooth = 6.0 * m - total

    for e in range(SWEEPS // 2):
        for i in range(4):
            wait_send(functools.partial(face, e), i)
        wait_lines_sent(e)
    for i in range(3):
        wait_send(const_copy, i)
    for i in range(3):
        wait_send(model_copy, i)

    owned = part[pl.ds(pl.multiple_of(pos[2] * rows, rows), rows), :]
    for d in range(1, n):
        rs_copy(d).wait_recv()
    for d in range(1, n):
        owned = owned + rs[d - 1]
    my = m.shape[1]
    for k in range(m.shape[0]):
        grad[k] = owned[k * my : (k + 1) * my] + smooth[k]

    for d in range(1, n):
        rs_copy(d).wait_send()


def flush(fields, grad, fields_hbm, grad_hbm, sem):
    copies = [
        pltpu.make_async_copy(fields, fields_hbm, sem.at[0]),
        pltpu.make_async_copy(grad, grad_hbm, sem.at[1]),
    ]
    for copy in copies:
        copy.start()
    for copy in copies:
        copy.wait()


def solution(mesh):
    sizes = tuple(mesh.shape[a] for a in AXES)

    def body(initial, source, classes, coupling, owner, model):
        chans, nx, ny, nz = initial.shape
        n = sizes[2]
        groups = n * model.size // nz
        dma = pltpu.SemaphoreType.DMA
        vmem = pl.BlockSpec(memory_space=pltpu.VMEM)
        hbm = pl.BlockSpec(memory_space=pltpu.HBM)
        results = pl.pallas_call(
            functools.partial(kernel, sizes),
            out_shape=(
                pltpu.VMEM(initial.shape, F32),
                pltpu.VMEM(model.shape, F32),
            ),
            in_specs=[hbm] * 6,
            out_specs=(vmem, vmem),
            scratch_shapes=[
                pltpu.VMEM(initial.shape, F32),
                pltpu.VMEM(source.shape, F32),
                pltpu.VMEM(classes.shape, jnp.int32),
                pltpu.SMEM(coupling.shape, F32),
                pltpu.VMEM(owner.shape, jnp.int32),
                pltpu.VMEM(model.shape, F32),
                pltpu.VMEM((SWEEPS - 1, chans, nx, ny, nz), F32),
                pltpu.VMEM((chans, nx, ny, nz), F32),
                pltpu.VMEM((chans + 2, nx, ny, nz), F32),
                pltpu.VMEM((nx, ny, nz), F32),
                pltpu.VMEM((chans, nx, ny, nz), F32),
                pltpu.VMEM((SWEEPS, 2, chans, 2, ny, nz), F32),
                pltpu.VMEM((SWEEPS, 2, 2, chans, nx, nz), F32),
                pltpu.VMEM((SWEEPS, 2, 2, 2, ny, nz), F32),
                pltpu.VMEM((SWEEPS // 2, 4, 16, nz), F32),
                pltpu.VMEM((SWEEPS // 2, 4, 2, ny, nz), F32),
                pltpu.VMEM((SWEEPS // 2, 4, 2, ny, nz), F32),
                pltpu.VMEM((2, chans + 2, ny, nz), F32),
                pltpu.VMEM((2, chans + 2, nx, nz), F32),
                pltpu.VMEM((2, 4, ny, nz), F32),
                pltpu.VMEM((SWEEPS, 2, 2, chans, nx, nz), F32),
                pltpu.VMEM((SWEEPS, 2, 2, ny, nz), F32),
                pltpu.VMEM((SWEEPS // 2, 4, 16, nz), F32),
                pltpu.VMEM((SWEEPS // 2, 2, ny, nz), F32),
                pltpu.VMEM((2, chans + 2, nx, nz), F32),
                pltpu.VMEM((4, ny, nz), F32),
                pltpu.VMEM((6,) + model.shape, F32),
                pltpu.VMEM((nz, nx * ny * nz), BF16),
                pltpu.VMEM((groups, nx * ny * nz), BF16),
                pltpu.VMEM((groups, nz), F32),
                pltpu.VMEM((n - 1, groups // n, nz), F32),
                dma((6,)),
                dma((SWEEPS // 2, 8)),
                dma((SWEEPS // 2, 8)),
                dma((SWEEPS // 2, 12)),
                dma((SWEEPS // 2, 12)),
                dma((6,)),
                dma((6,)),
                dma((6,)),
                dma((6,)),
                dma((n - 1,)),
                dma((n - 1,)),
            ],
            compiler_params=pltpu.CompilerParams(
                collective_id=0, has_side_effects=True, vmem_limit_bytes=60 * 1024 * 1024
            ),
        )(initial, source, classes, coupling, owner, model)
        return pl.pallas_call(
            flush,
            out_shape=(
                jax.ShapeDtypeStruct(initial.shape, F32),
                jax.ShapeDtypeStruct(model.shape, F32),
            ),
            in_specs=[vmem, vmem],
            out_specs=(hbm, hbm),
            scratch_shapes=[dma((2,))],
        )(*[pltpu.with_memory_space_constraint(r, pltpu.VMEM) for r in results])

    in_specs = (
        P(None, "gx", "gy", "gz"),
        P(None, "gx", "gy", "gz"),
        P("gx", "gy", "gz"),
        P(),
        P("gx", "gy", "gz"),
        P("gx", "gy", "gz"),
    )
    out_specs = (P(None, "gx", "gy", "gz"), P("gx", "gy", "gz"))
    return jax.shard_map(body, mesh=mesh, in_specs=in_specs, out_specs=out_specs, check_vma=False)
```

```python
import functools

import jax
import jax.numpy as jnp
from jax import lax
from jax.experimental import pallas as pl
from jax.experimental.pallas import tpu as pltpu
from jax.sharding import PartitionSpec as P

SWEEPS = 4
MESH = pl.DeviceIdType.MESH
AXES = ("gx", "gy", "gz")
F32 = jnp.float32
BF16 = jnp.bfloat16


def kernel(
    sizes, init_hbm, src_hbm, cls_hbm, coup_hbm, own_hbm, mod_hbm, out, grad,
    init, src, cls, coup, own, mod, f, part_next, const, kap, ycor,
    hx, hy, hz, hxy, hxz, hyz, hcx, hcy, hcz, sy, sz, sxy, syz, scy, scz,
    hm, lo_hot, hi_hot, part, rs,
    load_sem, send_sem, recv_sem, esend, erecv, csend, crecv, msend, mrecv, rsend, rrecv,
):
    chans, nx, ny, nz = init.shape
    pairs = chans // 2
    half = chans // 2
    per_vreg = chans * nx // 2
    pos = [lax.axis_index(a) for a in AXES]
    has = [(pos[i] > 0, pos[i] < sizes[i] - 1) for i in range(3)]
    n = sizes[2]
    peers = [lax.rem(pos[2] + d, n) for d in range(1, n)]
    ends = [[pos[i] - 1, pos[i] + 1] for i in range(3)]
    lines = [
        (m, i, j, si, sj)
        for m, (i, j) in enumerate(((0, 1), (0, 2), (1, 2)))
        for si in range(2)
        for sj in range(2)
    ]

    loads = [
        pltpu.make_async_copy(a, b, load_sem.at[k])
        for k, (a, b) in enumerate(
            (
                (init_hbm, init), (mod_hbm, mod), (cls_hbm, cls), (src_hbm, src), (own_hbm, own),
                (coup_hbm, coup),
            )
        )
    ]
    loads[0].start()
    barrier = pltpu.get_barrier_semaphore()
    for i in range(2):
        for side in range(2):

            @pl.when(has[i][side])
            def _():
                pl.semaphore_signal(
                    barrier, inc=1, device_id={AXES[i]: ends[i][side]}, device_id_type=MESH
                )

    for d in range(1, n):
        pl.semaphore_signal(barrier, inc=1, device_id={"gz": peers[d - 1]}, device_id_type=MESH)

    def met(i, j, si, sj):
        return jnp.logical_and(has[i][si], has[j][sj])

    for m, i, j, si, sj in lines:

        @pl.when(met(i, j, si, sj))
        def _():
            pl.semaphore_signal(
                barrier,
                inc=1,
                device_id={AXES[i]: ends[i][si], AXES[j]: ends[j][sj]},
                device_id_type=MESH,
            )

    greeted = n - 1
    for i in range(2):
        for side in range(2):
            greeted = greeted + has[i][side].astype(jnp.int32)
    for m, i, j, si, sj in lines:
        greeted = greeted + met(i, j, si, sj).astype(jnp.int32)

    for load in loads[1:]:
        load.start()

    lane = lax.broadcasted_iota(jnp.int32, (ny, nz), 1)
    sub = lax.broadcasted_iota(jnp.int32, (ny, nz), 0)
    even = (lane & 1) == 0
    shift3 = jnp.where(even, lane, lane - 3)
    xlane = (lane >> 1) % nx
    real = ((lane // (2 * nx)) & 1) == 0

    for i, halo in enumerate((hx, hy, hz)):
        for side in range(2):

            @pl.when(jnp.logical_not(has[i][side]))
            def _():
                halo[:, side] = jnp.zeros(halo.shape[:1] + halo.shape[2:], F32)
                hm[2 * i + side] = jnp.zeros(hm.shape[1:], F32)

    held = (hxy, hxz, hyz)
    for m, i, j, si, sj in lines:

        @pl.when(jnp.logical_not(met(i, j, si, sj)))
        def _():
            line = held[m]
            line[:, 2 * si + sj] = jnp.zeros(line.shape[:1] + line.shape[2:], F32)

    def face(e, i, side):
        s = 2 * e
        cells = init if e == 0 else f.at[s - 1]
        axis = min(i, 2)
        if i == 0:
            source = cells.at[:, pl.ds(0 if side == 0 else nx - 2, 2)]
            halo = hx.at[s, 1 - side]
        elif i == 2:
            source = sz.at[s]
            halo = hz.at[s, 1 - side]
        else:
            axis = 1
            mine = pl.ds(0 if i == 1 else half, half)
            source = sy.at[s, side, :, mine]
            halo = hy.at[s, 1 - side, :, mine]
        return pltpu.make_async_remote_copy(
            src_ref=source,
            dst_ref=halo,
            send_sem=send_sem.at[e, 2 * i + side],
            recv_sem=recv_sem.at[e, 2 * i + 1 - side],
            device_id={AXES[axis]: ends[axis][side]},
            device_id_type=MESH,
        )

    def line_copy(e, m, i, j, si, sj):
        s = 2 * e
        source = (sxy.at[e, 2 * si + sj], sz.at[s, :, 0], syz.at[e])[m]
        there = 2 * (1 - si) + 1 - sj
        return pltpu.make_async_remote_copy(
            src_ref=source,
            dst_ref=held[m].at[e, there],
            send_sem=esend.at[e, 4 * m + 2 * si + sj],
            recv_sem=erecv.at[e, 4 * m + there],
            device_id={AXES[i]: ends[i][si], AXES[j]: ends[j][sj]},
            device_id_type=MESH,
        )

    def start_lines(e):
        for m, i, j, si, sj in lines:

            @pl.when(met(i, j, si, sj))
            def _():
                line_copy(e, m, i, j, si, sj).start()

    def wait_lines(e):
        for m, i, j, si, sj in lines:

            @pl.when(met(i, j, si, sj))
            def _():
                line_copy(e, m, i, j, 1 - si, 1 - sj).wait_recv()

    def wait_lines_sent(e):
        for m, i, j, si, sj in lines:

            @pl.when(met(i, j, si, sj))
            def _():
                line_copy(e, m, i, j, si, sj).wait_send()

    def const_copy(i, side):
        if i == 0:
            source, halo = const.at[:, 0 if side == 0 else nx - 1], hcx
            halo = halo.at[1 - side]
        elif i == 2:
            source, halo = scz, hcz.at[1 - side]
        else:
            some = pl.ds(0, half + 2) if i == 1 else pl.ds(half + 2, half)
            source, halo = scy.at[side, some], hcy.at[1 - side, some]
        return pltpu.make_async_remote_copy(
            src_ref=source,
            dst_ref=halo,
            send_sem=csend.at[2 * i + side],
            recv_sem=crecv.at[2 * i + 1 - side],
            device_id={AXES[i % 2 if i == 3 else i]: ends[i % 2 if i == 3 else i][side]},
            device_id_type=MESH,
        )

    def model_copy(i, side):
        return pltpu.make_async_remote_copy(
            src_ref=mod,
            dst_ref=hm.at[2 * i + 1 - side],
            send_sem=msend.at[2 * i + side],
            recv_sem=mrecv.at[2 * i + 1 - side],
            device_id={AXES[i]: ends[i][side]},
            device_id_type=MESH,
        )

    def start(make, i):
        for side in range(2):

            @pl.when(has[i % 2 if i == 3 else i][side])
            def _():
                make(i, side).start()

    def wait_recv(make, i):
        for side in range(2):

            @pl.when(has[i % 2 if i == 3 else i][side])
            def _():
                make(i, 1 - side).wait_recv()

    def wait_send(make, i):
        for side in range(2):

            @pl.when(has[i % 2 if i == 3 else i][side])
            def _():
                make(i, side).wait_send()

    def channels_of(g):
        return range(g * half, g * half + half)

    def pack_z(acc, value, j):
        return jnp.where((lane >> 1) == j, pltpu.roll(value, 2 * j + 1, 1), acc)

    def pack_z2(acc, value, j):
        return jnp.where(shift3 == 2 * j, pltpu.roll(value, 2 * j + 2, 1), acc)

    def pack_rows(cells, s, g, layer=0):
        flat = cells.reshape(chans * nx * ny, nz)
        for c in channels_of(g):
            for side, row in enumerate((layer, ny - 1 - layer)):
                sy[s, side, layer, c] = flat[pl.ds(c * nx * ny + row, nx, stride=ny), :]

    def pack_lines(e):
        s = 2 * e
        acc = jnp.zeros((nx, nz), F32)
        for c in range(chans):
            for side in range(2):
                acc = pack_z(acc, sy[s, side, 0, c], 2 * c + side)
        syz[e, 0] = acc
        for g in range(2):
            for side, row in enumerate((0, ny - 1)):
                at = 2 * side + g
                syz[e, 1, at : at + 1, :] = sz[s, g, 0, row : row + 1, :]
        for side in range(2):
            flat = sy.at[s, side, 0].reshape(chans * nx, nz)
            for end, x in enumerate((0, nx - 1)):
                sxy[e, 2 * end + side, 0:chans] = flat[pl.ds(x, chans, stride=nx), :]

    loads[0].wait()
    for g in range(2):
        pack_rows(init, 0, g)
        pack_rows(init, 0, g, 1)
        acc = jnp.zeros((ny, nz), F32)
        acc2 = jnp.zeros((ny, nz), F32)
        for j in range(per_vreg):
            c, x = divmod(g * per_vreg + j, nx)
            cell = init[c, x]
            acc = pack_z(acc, cell, j)
            acc2 = pack_z2(acc2, cell, j)
        sz[0, g, 0] = acc
        sz[0, g, 1] = acc2
    pack_lines(0)

    pl.semaphore_wait(barrier, greeted)
    for i in (1, 2, 0):
        start(functools.partial(face, 0), i)
    start_lines(0)

    loads[2].wait()
    loads[5].wait()
    loads[3].wait()
    classes = cls[...]
    kappa = jnp.zeros(classes.shape, F32)
    for k in range(coup.shape[0]):
        kappa = jnp.where(classes == k, coup[k], kappa)
    scale = 0.8 / (36.0 + kappa * kappa)
    const[chans] = 6.0 * scale
    const[chans + 1] = kappa * scale
    kap[...] = kappa

    def shifted(v):
        zero = jnp.zeros((1, ny, nz), F32)
        total = jnp.concatenate([zero, v[:-1]], 0) + jnp.concatenate([v[1:], zero], 0)
        total = total + (pltpu.roll(v, 1, 1) + pltpu.roll(v, ny - 1, 1))
        return total + (pltpu.roll(v, 1, 2) + pltpu.roll(v, nz - 1, 2))

    def local(s, g):
        cells = init if s == 0 else f.at[s - 1]

        def one(p, carry):
            a, b = const[chans], const[chans + 1]
            fr, fi = cells[2 * p], cells[2 * p + 1]
            cr, ci = const[2 * p], const[2 * p + 1]
            tr, ti = shifted(fr), shifted(fi)
            part_next[2 * p] = cr + 0.2 * fr + (a * tr + b * ti)
            part_next[2 * p + 1] = ci + 0.2 * fi + (a * ti - b * tr)
            return carry

        lax.fori_loop(g * pairs // 2, (g + 1) * pairs // 2, one, 0, unroll=True)

    ycor[...] = jnp.zeros(ycor.shape, F32)

    def merge(low, high):
        return jnp.where(even, low, pltpu.roll(high, nz - 2, 1))

    def finish(s, g):
        cells = out if s == SWEEPS - 1 else f.at[s]
        last = s == SWEEPS - 1
        deep = s % 2 == 1 and not last
        own_z = sz[s, g, 0]
        merged = merge(hz[s, 0, g, 0] - own_z, hz[s, 1, g, 0] - own_z)
        edge = (lane == 0) | (lane == nz - 1)
        rows = ycor.reshape(chans * nx * ny, nz)
        for c in channels_of(g):
            for side, row in ((0, 0), (1, ny - 1)):
                rows[pl.ds(c * nx * ny + row, nx, stride=ny), :] = (
                    hy[s, side, 0, c] - sy[s, 1 - side, 0, c]
                )

        def one(q, accs):
            acc, acc2 = accs
            c = g * half + 2 * q
            for x in range(nx):
                sums = []
                for r in range(2):
                    j = (2 * q + r) * nx + x
                    h = ycor[c + r, x] + jnp.where(edge, pltpu.roll(merged, nz - 2 * j, 1), 0.0)
                    if x == 0:
                        h = h + hx[s, 0, c + r, 1]
                    if x == nx - 1:
                        h = h + hx[s, 1, c + r, 0]
                    sums.append(h)
                a, b = const[chans, x], const[chans + 1, x]
                nr = part_next[c, x] + (a * sums[0] + b * sums[1])
                ni = part_next[c + 1, x] + (a * sums[1] - b * sums[0])
                cells[c, x] = nr
                cells[c + 1, x] = ni
                for r, value in enumerate((nr, ni)):
                    j = (2 * q + r) * nx + x
                    if not last:
                        acc = pack_z(acc, value, j)
                    if deep:
                        acc2 = pack_z2(acc2, value, j)
            return acc, acc2

        zero = jnp.zeros((ny, nz), F32)
        acc, acc2 = lax.fori_loop(0, pairs // 2, one, (zero, zero), unroll=True)
        if not last:
            sz[s + 1, g, 0] = acc
        if deep:
            sz[s + 1, g, 1] = acc2

    def stepped(fixed, field, total, a, b):
        tr, ti = total
        return (
            fixed[0] + 0.2 * field[0] + (a * tr + b * ti),
            fixed[1] + 0.2 * field[1] + (a * ti - b * tr),
        )

    def around(field, low, high, ends_z):
        count = field.shape[0]
        total = jnp.where(sub == 0, low, pltpu.roll(field, 1, 0))
        total = total + jnp.where(sub == count - 1, high, pltpu.roll(field, count - 1, 0))
        total = total + jnp.where(lane == 0, ends_z, pltpu.roll(field, 1, 1))
        return total + jnp.where(lane == nz - 1, ends_z, pltpu.roll(field, nz - 1, 1))

    def spread(row, count):
        return jnp.broadcast_to(row, (count, nz))

    def kept(i, side, value):
        return jnp.where(has[i][side], value, 0.0)

    def outer(e, only):
        s = 2 * e
        cells = init if e == 0 else f.at[s - 1]
        both = [(g, side) for g in only for side in range(2)]

        for g, side in both:
            v = hz[s, side, g, 0]
            second = hz[s, side, g, 1]
            if side == 1:
                second = pltpu.roll(second, nz - 2, 1)
            mine = pltpu.roll(sz[s, g, 0], nz - 1 if side == 0 else 1, 1)
            low = spread(hyz[e, side, 1, 2 + g : 3 + g, :], ny)
            high = spread(hyz[e, 2 + side, 1, g : g + 1, :], ny)
            t = second + mine
            t = t + jnp.where(sub == 0, low, pltpu.roll(v, 1, 0))
            t = t + jnp.where(sub == ny - 1, high, pltpu.roll(v, ny - 1, 0))
            over = 2 * (nx - 1)
            t = t + jnp.where(
                xlane == 0, pltpu.roll(hxz[e, side, g], nz - over, 1), pltpu.roll(v, 2, 1)
            )
            t = t + jnp.where(
                xlane == nx - 1,
                pltpu.roll(hxz[e, 2 + side, g], over, 1),
                pltpu.roll(v, nz - 2, 1),
            )
            other = jnp.where(real, pltpu.roll(t, nz - 2 * nx, 1), -pltpu.roll(t, 2 * nx, 1))
            new = hcz[side, g] + 0.2 * v + (hcz[side, 2] * t + hcz[side, 3] * other)
            hz[s + 1, side, g, 0] = kept(2, side, new)

        for g, side in both:
            ends_z = merge(hyz[e, 2 * side, 0], hyz[e, 2 * side + 1, 0])
            a, b = hcy[side, 0], hcy[side, 1]
            for q in range(half // 2):
                c = g * half + 2 * q
                fields, totals = [], []
                for r in range(2):
                    j = 2 * (c + r) + 1 - side
                    v = hy[s, side, 0, c + r]
                    low = spread(hxy[e, side, c + r : c + r + 1, :], nx)
                    high = spread(hxy[e, 2 + side, c + r : c + r + 1, :], nx)
                    t = around(v, low, high, pltpu.roll(ends_z, (nz - 2 * j) % nz, 1))
                    fields.append(v)
                    totals.append(t + hy[s, side, 1, c + r] + sy[s, side, 0, c + r])
                nr, ni = stepped((hcy[side, c + 2], hcy[side, c + 3]), fields, totals, a, b)
                hy[s + 1, side, 0, c] = kept(1, side, nr)
                hy[s + 1, side, 0, c + 1] = kept(1, side, ni)

        for g, side in both:
            one, two = (1, 0) if side == 0 else (0, 1)
            x = 0 if side == 0 else nx - 1
            ends_z = merge(hxz[e, 2 * side, g], hxz[e, 2 * side + 1, g])
            a, b = hcx[side, chans], hcx[side, chans + 1]
            for q in range(half // 2):
                c = g * half + 2 * q
                fields, totals = [], []
                for r in range(2):
                    j = (2 * q + r) * nx + (nx - 1 - x)
                    v = hx[s, side, c + r, one]
                    low = spread(hxy[e, 2 * side, c + r : c + r + 1, :], ny)
                    high = spread(hxy[e, 2 * side + 1, c + r : c + r + 1, :], ny)
                    t = around(v, low, high, pltpu.roll(ends_z, (nz - 2 * j) % nz, 1))
                    fields.append(v)
                    totals.append(t + hx[s, side, c + r, two] + cells[c + r, x])
                nr, ni = stepped((hcx[side, c], hcx[side, c + 1]), fields, totals, a, b)
                hx[s + 1, side, c, one] = kept(0, side, nr)
                hx[s + 1, side, c + 1, one] = kept(0, side, ni)

    groups = hi_hot.shape[0]

    def hots(x0, x1):
        rows = lax.broadcasted_iota(jnp.int32, (16, nz), 0)
        bands = [(rows + 16 * k).astype(F32).astype(BF16) for k in range(max(nz, groups) // 16)]
        yes, no = jnp.ones((16, nz), BF16), jnp.zeros((16, nz), BF16)

        def one(x, carry):
            for y in range(ny):
                v = own[x, y : y + 1, :]
                at = pl.ds(pl.multiple_of((x * ny + y) * nz, nz), nz)
                low = jnp.broadcast_to((v & (nz - 1)).astype(F32), (16, nz)).astype(BF16)
                high = jnp.broadcast_to((v >> 7).astype(F32), (16, nz)).astype(BF16)
                for k in range(nz // 16):
                    lo_hot[16 * k : 16 * k + 16, at] = jnp.where(bands[k] == low, yes, no)
                for k in range(groups // 16):
                    hi_hot[16 * k : 16 * k + 16, at] = jnp.where(bands[k] == high, yes, no)
            return carry

        lax.fori_loop(x0, x1, one, 0, unroll=True)

    loads[4].wait()
    flat = const.reshape((chans + 2) * nx * ny, nz)

    def pack_const(into, c):
        for side, row in enumerate((0, ny - 1)):
            scy[side, into] = flat[pl.ds(c * nx * ny + row, nx, stride=ny), :]

    a, b = const[chans], const[chans + 1]
    for r in range(2):
        pack_const(r, chans + r)
    for g in range(2):
        for c in range(g * half, g * half + half, 2):
            sr, si = src[c], src[c + 1]
            const[c] = a * sr + b * si
            const[c + 1] = a * si - b * sr
            pack_const(c + 2, c)
            pack_const(c + 3, c + 1)
        if g == 0:
            start(const_copy, 1)
            start(functools.partial(face, 0), 3)
        else:
            start(const_copy, 3)
            start(const_copy, 0)
    for g in range(4):
        acc = jnp.zeros((ny, nz), F32)
        for j in range(per_vreg if g < 2 else nx):
            c, x = divmod(g * per_vreg + j, nx) if g < 2 else (chans + g - 2, j)
            acc = pack_z(acc, const[c, x], j)
        block = 2 * nx
        while g >= 2 and block < nz:
            acc = acc + pltpu.roll(acc, block, 1)
            block *= 2
        scz[g] = acc
    start(const_copy, 2)
    loads[1].wait()
    for i in range(3):
        start(model_copy, i)
    for g in range(2):
        local(0, g)
    hots(0, nx // 2)
    def first(e, g):
        s = 2 * e
        for i in (1, 0, 2) if g == 0 else (3,):
            wait_recv(functools.partial(face, e), i)
        finish(s, g)
        pack_rows(f.at[s], s + 1, g)
        local(s + 1, g)

    def second(e, g):
        s = 2 * e
        if e == 0:
            for i in (0, 2, 1) if g == 0 else (3,):
                wait_recv(const_copy, i)
        if g == 0:
            wait_lines(e)
        outer(e, (g,))
        finish(s + 1, g)
        if s + 2 < SWEEPS:
            pack_rows(f.at[s + 1], s + 2, g)
            pack_rows(f.at[s + 1], s + 2, g, 1)
            start(functools.partial(face, e + 1), 1 + 2 * g)

    for e in range(SWEEPS // 2):
        s = 2 * e
        if e == 0:
            for g in range(2):
                first(e, g)
                second(e, g)
        else:
            for g in range(2):
                first(e, g)
            for g in range(2):
                second(e, g)
        if s + 2 < SWEEPS:
            for i in (2, 0):
                start(functools.partial(face, e + 1), i)
            pack_lines(e + 1)
            start_lines(e + 1)
            for g in range(2):
                local(s + 2, g)
            if e == 0:
                hots(nx // 2, nx)

    def plane(x, total):
        sens = jnp.zeros((ny, nz), F32)
        for k in range(pairs // 2):
            fr, fi = out[2 * k, x], out[2 * k + 1, x]
            gr, gi = out[pairs + 2 * k, x], out[pairs + 2 * k + 1, x]
            sens = sens + (fr * gi + fi * gr)
        sens = kap[x] * sens
        s0 = sens.astype(BF16).astype(F32)
        rest = sens - s0
        s1 = rest.astype(BF16).astype(F32)
        s2 = rest - s1
        left = []
        for piece in (s0, s1, s2):
            row = jnp.concatenate(
                [jnp.broadcast_to(piece[y : y + 1, :], (groups, nz)) for y in range(ny)], 1
            ).astype(BF16)
            left.append(row)
        at = pl.ds(pl.multiple_of(x * ny * nz, nz), ny * nz)
        hi = hi_hot[:, at]
        lhs = jnp.concatenate([hi * row for row in left], 0)
        return total + lax.dot_general(
            lhs, lo_hot[:, at], (((1,), (1,)), ((), ())), preferred_element_type=F32
        )

    total = lax.fori_loop(0, nx, plane, jnp.zeros((3 * groups, nz), F32), unroll=True)
    part[...] = total[:groups] + total[groups : 2 * groups] + total[2 * groups :]

    rows = groups // n

    def rs_copy(d):
        return pltpu.make_async_remote_copy(
            src_ref=part.at[pl.ds(pl.multiple_of(peers[d - 1] * rows, rows), rows)],
            dst_ref=rs.at[d - 1],
            send_sem=rsend.at[d - 1],
            recv_sem=rrecv.at[d - 1],
            device_id={"gz": peers[d - 1]},
            device_id_type=MESH,
        )

    for d in range(1, n):
        rs_copy(d).start()

    for i in range(3):
        wait_recv(model_copy, i)
    m = mod[...]
    mz = m.shape[2]
    mlane = lax.broadcasted_iota(jnp.int32, m.shape, 2)
    total = jnp.concatenate([hm[0][-1:], m[:-1]], 0) + jnp.concatenate([m[1:], hm[1][:1]], 0)
    total = total + jnp.concatenate([hm[2][:, -1:], m[:, :-1]], 1)
    total = total + jnp.concatenate([m[:, 1:], hm[3][:, :1]], 1)
    total = total + pltpu.roll(jnp.where(mlane == mz - 1, hm[4], m), 1, 2)
    total = total + pltpu.roll(jnp.where(mlane == 0, hm[5], m), mz - 1, 2)
    smooth = 6.0 * m - total

    for e in range(SWEEPS // 2):
        for i in range(4):
            wait_send(functools.partial(face, e), i)
        wait_lines_sent(e)
    for i in range(4):
        wait_send(const_copy, i)
    for i in range(3):
        wait_send(model_copy, i)

    owned = part[pl.ds(pl.multiple_of(pos[2] * rows, rows), rows), :]
    for d in range(1, n):
        rs_copy(d).wait_recv()
    for d in range(1, n):
        owned = owned + rs[d - 1]
    my = m.shape[1]
    for k in range(m.shape[0]):
        grad[k] = owned[k * my : (k + 1) * my] + smooth[k]

    for d in range(1, n):
        rs_copy(d).wait_send()


def flush(fields, grad, fields_hbm, grad_hbm, sem):
    copies = [
        pltpu.make_async_copy(fields, fields_hbm, sem.at[0]),
        pltpu.make_async_copy(grad, grad_hbm, sem.at[1]),
    ]
    for copy in copies:
        copy.start()
    for copy in copies:
        copy.wait()


def solution(mesh):
    sizes = tuple(mesh.shape[a] for a in AXES)

    def body(initial, source, classes, coupling, owner, model):
        chans, nx, ny, nz = initial.shape
        n = sizes[2]
        groups = n * model.size // nz
        dma = pltpu.SemaphoreType.DMA
        vmem = pl.BlockSpec(memory_space=pltpu.VMEM)
        hbm = pl.BlockSpec(memory_space=pltpu.HBM)
        results = pl.pallas_call(
            functools.partial(kernel, sizes),
            out_shape=(
                pltpu.VMEM(initial.shape, F32),
                pltpu.VMEM(model.shape, F32),
            ),
            in_specs=[hbm] * 6,
            out_specs=(vmem, vmem),
            scratch_shapes=[
                pltpu.VMEM(initial.shape, F32),
                pltpu.VMEM(source.shape, F32),
                pltpu.VMEM(classes.shape, jnp.int32),
                pltpu.SMEM(coupling.shape, F32),
                pltpu.VMEM(owner.shape, jnp.int32),
                pltpu.VMEM(model.shape, F32),
                pltpu.VMEM((SWEEPS - 1, chans, nx, ny, nz), F32),
                pltpu.VMEM((chans, nx, ny, nz), F32),
                pltpu.VMEM((chans + 2, nx, ny, nz), F32),
                pltpu.VMEM((nx, ny, nz), F32),
                pltpu.VMEM((chans, nx, ny, nz), F32),
                pltpu.VMEM((SWEEPS, 2, chans, 2, ny, nz), F32),
                pltpu.VMEM((SWEEPS, 2, 2, chans, nx, nz), F32),
                pltpu.VMEM((SWEEPS, 2, 2, 2, ny, nz), F32),
                pltpu.VMEM((SWEEPS // 2, 4, 16, nz), F32),
                pltpu.VMEM((SWEEPS // 2, 4, 2, ny, nz), F32),
                pltpu.VMEM((SWEEPS // 2, 4, 2, ny, nz), F32),
                pltpu.VMEM((2, chans + 2, ny, nz), F32),
                pltpu.VMEM((2, chans + 2, nx, nz), F32),
                pltpu.VMEM((2, 4, ny, nz), F32),
                pltpu.VMEM((SWEEPS, 2, 2, chans, nx, nz), F32),
                pltpu.VMEM((SWEEPS, 2, 2, ny, nz), F32),
                pltpu.VMEM((SWEEPS // 2, 4, 16, nz), F32),
                pltpu.VMEM((SWEEPS // 2, 2, ny, nz), F32),
                pltpu.VMEM((2, chans + 2, nx, nz), F32),
                pltpu.VMEM((4, ny, nz), F32),
                pltpu.VMEM((6,) + model.shape, F32),
                pltpu.VMEM((nz, nx * ny * nz), BF16),
                pltpu.VMEM((groups, nx * ny * nz), BF16),
                pltpu.VMEM((groups, nz), F32),
                pltpu.VMEM((n - 1, groups // n, nz), F32),
                dma((6,)),
                dma((SWEEPS // 2, 8)),
                dma((SWEEPS // 2, 8)),
                dma((SWEEPS // 2, 12)),
                dma((SWEEPS // 2, 12)),
                dma((8,)),
                dma((8,)),
                dma((6,)),
                dma((6,)),
                dma((n - 1,)),
                dma((n - 1,)),
            ],
            compiler_params=pltpu.CompilerParams(
                collective_id=0, has_side_effects=True, vmem_limit_bytes=60 * 1024 * 1024
            ),
        )(initial, source, classes, coupling, owner, model)
        return pl.pallas_call(
            flush,
            out_shape=(
                jax.ShapeDtypeStruct(initial.shape, F32),
                jax.ShapeDtypeStruct(model.shape, F32),
            ),
            in_specs=[vmem, vmem],
            out_specs=(hbm, hbm),
            scratch_shapes=[dma((2,))],
        )(*[pltpu.with_memory_space_constraint(r, pltpu.VMEM) for r in results])

    in_specs = (
        P(None, "gx", "gy", "gz"),
        P(None, "gx", "gy", "gz"),
        P("gx", "gy", "gz"),
        P(),
        P("gx", "gy", "gz"),
        P("gx", "gy", "gz"),
    )
    out_specs = (P(None, "gx", "gy", "gz"), P("gx", "gy", "gz"))
    return jax.shard_map(body, mesh=mesh, in_specs=in_specs, out_specs=out_specs, check_vma=False)
```
